128 devices in a mesh: dp: 8 (over z_lo, y), fsdp: 16 (over z_hi, x, core).
Axes of the slice: x: 4, y: 4, z: 4 (z_hi: 2, z_lo: 2; z = z_hi * 2 + z_lo), core: 2. Of those that a mesh axis runs over, the one named last changes fastest.
Arguments:
- queries: bfloat16 [16384, 4096], P(('dp', 'fsdp')), may hold values from -70 to 70
- keys: bfloat16 [16384, 512], P(('dp', 'fsdp')), may hold values from -6 to 6
- values: bfloat16 [16384, 512], P(('dp', 'fsdp')), may hold values from -6 to 6
- output_gradient: bfloat16 [16384, 4096], P(('dp', 'fsdp')), may hold values from -6 to 6
- doc_lengths: int32 [8, 8], replicated, may hold values from 1 to 1024, 2048 in all within a row
- block_order: int32 [8, 128], replicated, may hold values from 0 to 127, each once within a row
- group_shift: int32 [16, 8], replicated, may hold values from 0 to 7, each once within a row
Outputs:
- attn_out: bfloat16 [16384, 4096], P(('dp', 'fsdp'))
- grad_q: bfloat16 [16384, 4096], P(('dp', 'fsdp'))
- grad_k: bfloat16 [16384, 512], P(('dp', 'fsdp'))
- grad_v: bfloat16 [16384, 512], P(('dp', 'fsdp'))
The draws below stay inside these ranges and needn't reach their ends.
Inputs may be any that keep to these rules, and one draw needn't show every extreme that they name: `doc_lengths`: each row holds the lengths of the 8 documents of one group in position order; a row sums to 2048 and its largest entry is 1024. `block_order`: each row is a permutation. `group_shift`: each row is a permutation.
All inputs are finite; a program needn't handle non-finite values.
Results may differ from the reference program's by a relative error of at most 0.03.
Values may be sent and summed in bfloat16 or wider, within the bound.
A program may use at most 128 MiB of HBM per device.

```python
import math
import jax
import jax.numpy as jnp
import numpy as np
from jax import lax

HQ = 32
KEY_HEADS = 4
HEAD_SIZE = 128
QUERY_PER_KEY = 8
TOK_DEV = 128
NDOC = 8
BLOCK = 16
GROUP_ROWS = 2048
NBLK = 128
LONGEST = 1024
TOKEN_COUNT = 16384
N_DP = 8
N_FSDP = 16


def draw_queries(key, part):
    key = jax.random.fold_in(key, 11)
    shape = (TOKEN_COUNT, HQ * HEAD_SIZE)
    return jnp.clip(jax.random.normal(key, shape, jnp.float32), -6.0, 6.0).astype(jnp.bfloat16)


def block_scale(rng, extent, pieces, smallest, largest):
    gain = 1.0
    for position, blocks in pieces:
        heights = jax.random.uniform(jax.random.fold_in(jax.random.fold_in(rng, 6), position), (blocks,), jnp.float32, smallest / len(pieces), largest / len(pieces))
        gain = gain * jnp.repeat(jnp.exp(heights), extent[position] // blocks).reshape((-1,) + (1,) * (len(extent) - 1 - position))
    return gain


def length_profile(amount, total, most, skew):
    weights = [(1 << 20) // math.isqrt(standing ** skew) + 1 for standing in range(2, amount + 1)]
    spare, counts = total - most - (amount - 1), [1] * (amount - 1)
    while spare > 0:
        candidates = [i for i in range(amount - 1) if counts[i] < most]
        pool, budget = sum([weights[i] for i in candidates]), spare
        for i in candidates:
            addition = min(most - counts[i], max(1, budget * weights[i] // pool), spare)
            counts[i] = counts[i] + addition
            spare = spare - addition
    return np.array([most] + counts)


def ragged_sizes(own_key, number_of, total, most, lean):
    if number_of == 2:
        one = jax.random.randint(own_key, (), max(1, total - most), min(most, total - 1) + 1)
        return jnp.stack([one, total - one])
    tallies = jnp.asarray(length_profile(number_of, total, most, lean), jnp.int32)
    pairs = (number_of - 1) // 2
    donor, receiver = tallies[1:1 + 2 * pairs:2], tallies[2:2 + 2 * pairs:2]
    margin = jnp.minimum(donor - 1, most - receiver)
    shifted = jax.random.randint(jax.random.fold_in(own_key, 1), (pairs,), 0, 1 << 20) % (margin + 1)
    tallies = tallies.at[1:1 + 2 * pairs:2].set(donor - shifted).at[2:2 + 2 * pairs:2].set(receiver + shifted)
    return tallies[jax.random.permutation(jax.random.fold_in(own_key, 2), number_of)]


def centred(rng, shape, scale, most, shards=(), held_as=jnp.bfloat16):
    level = block_scale(rng, shape, shards, -0.22, 0.18) if shards else 1.0
    values = jax.random.normal(rng, shape, jnp.float32) * scale * level
    return jnp.minimum(jnp.maximum(values, -most), most).astype(held_as)


def setup_inputs(seed: int = 0) -> dict:
    key_of = jax.random.split(jax.random.key(seed), 8)
    return {
        "queries": draw_queries(jax.random.fold_in(key_of[7], 71), 0),
        "keys": centred(key_of[1], (TOKEN_COUNT, KEY_HEADS * HEAD_SIZE), 1.0, 6.0, ((0, 128),)),
        "values": centred(key_of[2], (TOKEN_COUNT, KEY_HEADS * HEAD_SIZE), 1.0, 6.0, ((0, 128),)),
        "output_gradient": centred(key_of[3], (TOKEN_COUNT, HQ * HEAD_SIZE), 1.0, 6.0, ((0, 128),)),
        "doc_lengths": jax.vmap(lambda own: ragged_sizes(own, NDOC, GROUP_ROWS, LONGEST, 2))(jax.random.split(key_of[4], N_DP)).reshape((N_DP, NDOC)).astype(jnp.int32),
        "block_order": jax.vmap(lambda own: jax.random.permutation(own, NBLK))(jax.random.split(key_of[5], N_DP)).reshape((N_DP, NBLK)).astype(jnp.int32),
        "group_shift": jax.vmap(lambda own: jax.random.permutation(own, N_DP))(jax.random.split(key_of[6], N_FSDP)).reshape((N_FSDP, N_DP)).astype(jnp.int32),
    }


NEGATIVE_FILL = -1.0e30


def move_rows(source, group_shift):
    width = source.shape[1]
    block_len = TOK_DEV // N_DP
    tiled = source.reshape(N_DP, N_FSDP, N_DP, block_len, width)
    group_ids = jnp.arange(N_DP, dtype=jnp.int32)[:, None, None]
    member_ids = jnp.arange(N_FSDP, dtype=jnp.int32)[None, :, None]
    block_ids = jnp.arange(N_DP, dtype=jnp.int32)[None, None, :]
    anchor = ((group_ids - group_shift[None, :, :]) % N_DP).astype(jnp.int32)
    return tiled[anchor, member_ids, block_ids].reshape(N_DP, GROUP_ROWS, width)


def low(tensor):
    return lax.optimization_barrier(tensor.astype(jnp.bfloat16)).astype(jnp.float32)


def group_pass(entries):
    group_query, group_key, group_value, group_gradient, group_pos, group_start = entries
    allowed = (group_pos[None, :] >= group_start[:, None]) & (group_pos[None, :] <= group_pos[:, None])
    scaling = 1.0 / (HEAD_SIZE ** 0.5)
    query_heads = group_query.reshape(GROUP_ROWS, KEY_HEADS, QUERY_PER_KEY, HEAD_SIZE).transpose(1, 2, 0, 3)
    gradient_heads = group_gradient.reshape(GROUP_ROWS, KEY_HEADS, QUERY_PER_KEY, HEAD_SIZE).transpose(1, 2, 0, 3)
    key_head_rows = group_key.reshape(GROUP_ROWS, KEY_HEADS, HEAD_SIZE).transpose(1, 0, 2)
    value_head_rows = group_value.reshape(GROUP_ROWS, KEY_HEADS, HEAD_SIZE).transpose(1, 0, 2)

    def one_head(head_items):
        q_part, k_part, v_part, g_part = head_items
        q_wide = q_part.astype(jnp.float32)
        k_wide = k_part.astype(jnp.float32)
        v_wide = v_part.astype(jnp.float32)
        g_wide = g_part.astype(jnp.float32)
        scores = jnp.einsum("gqd,kd->gqk", q_wide, k_wide) * scaling
        scores = jnp.where(allowed[None], scores, NEGATIVE_FILL)
        row_max = jnp.max(scores, axis=-1, keepdims=True)
        raw = jnp.where(allowed[None], jnp.exp(scores - row_max), 0.0)
        total = jnp.sum(raw, axis=-1, keepdims=True)
        attended = jnp.einsum("gqk,kd->gqd", low(raw), v_wide) / total
        attended = attended.astype(jnp.bfloat16)
        log_total = row_max + jnp.log(total)
        row_delta = jnp.sum(g_wide * attended.astype(jnp.float32), axis=-1, keepdims=True)
        probs = jnp.where(allowed[None], jnp.exp(scores - log_total), 0.0)
        dprob = jnp.einsum("gqd,kd->gqk", g_wide, v_wide)
        dscore = low(probs * (dprob - row_delta))
        grad_query = (jnp.einsum("gqk,kd->gqd", dscore, k_wide) * scaling).astype(jnp.bfloat16)
        key_gradient = (jnp.einsum("gqk,gqd->kd", dscore, q_wide) * scaling).astype(jnp.bfloat16)
        value_gradient = jnp.einsum("gqk,gqd->kd", low(probs), g_wide).astype(jnp.bfloat16)
        return attended, grad_query, key_gradient, value_gradient

    attended, grad_query, key_gradient, value_gradient = lax.map(one_head, (query_heads, key_head_rows, value_head_rows, gradient_heads))
    attended = attended.transpose(2, 0, 1, 3).reshape(GROUP_ROWS, HQ * HEAD_SIZE)
    grad_query = grad_query.transpose(2, 0, 1, 3).reshape(GROUP_ROWS, HQ * HEAD_SIZE)
    key_gradient = key_gradient.transpose(1, 0, 2).reshape(GROUP_ROWS, KEY_HEADS * HEAD_SIZE)
    value_gradient = value_gradient.transpose(1, 0, 2).reshape(GROUP_ROWS, KEY_HEADS * HEAD_SIZE)
    return attended, grad_query, key_gradient, value_gradient


def reference(queries, keys, values, output_gradient, doc_lengths, block_order, group_shift):
    moved_q = move_rows(queries, group_shift)
    moved_k = move_rows(keys, group_shift)
    moved_v = move_rows(values, group_shift)
    grads_in = output_gradient.reshape(N_DP, GROUP_ROWS, HQ * HEAD_SIZE)
    offsets = jnp.arange(BLOCK, dtype=jnp.int32)
    slot_pos = (block_order[:, :, None] * BLOCK + offsets[None, None, :]).reshape(N_DP, GROUP_ROWS).astype(jnp.int32)
    doc_ends = jnp.cumsum(doc_lengths, axis=1).astype(jnp.int32)
    slot_start = jnp.sum(jnp.where(doc_ends[:, None, :] <= slot_pos[:, :, None], doc_lengths[:, None, :], 0), axis=2).astype(jnp.int32)
    attended, grad_query, key_gradient, value_gradient = lax.map(group_pass, (moved_q, moved_k, moved_v, grads_in, slot_pos, slot_start))
    return (attended.reshape(TOKEN_COUNT, HQ * HEAD_SIZE), grad_query.reshape(TOKEN_COUNT, HQ * HEAD_SIZE),
            key_gradient.reshape(TOKEN_COUNT, KEY_HEADS * HEAD_SIZE), value_gradient.reshape(TOKEN_COUNT, KEY_HEADS * HEAD_SIZE))
```

```python
import functools
import math

import jax
import jax.numpy as jnp
from jax import lax
from jax.experimental import pallas as pl
from jax.experimental.pallas import tpu as pltpu
from jax.sharding import PartitionSpec as P

HEADS = 32
KEY_HEADS = 4
HEAD = 128
PER_KEY = 8
BLOCK = 16
ROWS = 128
GROUPS = 8
MEMBERS = 16
CHIPS = 8
GROUP_ROWS = 2048
HALF = HEADS * HEAD // 2
KEYS_HALF = KEY_HEADS * HEAD // 2
CHUNK = 128
MOST_CHUNKS = 9
SCALE = 1.0 / math.sqrt(HEAD)
LOG2E = 1.4426950408889634
FILL = -1e30
MESH = pl.DeviceIdType.MESH
MIB = 1 << 20


def place():
    group = lax.axis_index("dp")
    member = lax.axis_index("fsdp")
    return group, member // 8, (member // 2) % 4, member % 2


def member_of(zh, x, core):
    return zh * 8 + x * 2 + core


def gather_kernel(
    q_ref, k_ref, v_ref, do_ref, shift_ref, order_ref,
    rq_ref, do2_ref, kv_ref, table_ref,
    send_q, send_kv, q_ssem, q_rsem, kv_ssem, kv_rsem, do_ssem, do_rsem, g_ssem, g_rsem, local_sem,
):
    group, zh, x, core = place()
    member = member_of(zh, x, core)
    chip = zh * 4 + x
    right, left = (x + 1) % 4, (x + 3) % 4
    other = 1 - core
    z_peer = (group, member_of(1 - zh, x, core))
    r_peer = (group, member_of(zh, right, core))
    l_peer = (group, member_of(zh, left, core))
    core_peer = (group, member_of(zh, x, other))

    barrier = pltpu.get_barrier_semaphore()
    greeted = 0
    for dev in (z_peer, r_peer, l_peer, core_peer):
        pl.semaphore_signal(barrier, inc=1, device_id=dev, device_id_type=MESH)
        greeted += 1
    for step in range(1, GROUPS):
        for side in range(2):
            dev = ((group + GROUPS - step) % GROUPS, member_of(zh, x, side))
            pl.semaphore_signal(barrier, inc=1, device_id=dev, device_id_type=MESH)
            greeted += 1

    def block_for(row, step):
        found = jnp.int32(0)
        for b in range(GROUPS):
            found = jnp.maximum(found, jnp.where(shift_ref[row, b] == step, b, 0))
        return found

    for step in range(GROUPS):
        b = block_for(member, step)
        for side in range(2):
            cols = slice(side * KEYS_HALF, (side + 1) * KEYS_HALF)
            send_kv[step, side, :, 0:KEYS_HALF] = k_ref[b, :, cols]
            send_kv[step, side, :, KEYS_HALF:] = v_ref[b, :, cols]

    pl.semaphore_wait(barrier, greeted)

    def kv_copy(step, flip):
        side = core if flip == 0 else other
        return pltpu.make_async_remote_copy(
            src_ref=send_kv.at[step, side],
            dst_ref=kv_ref.at[chip, core, step],
            send_sem=kv_ssem.at[step, flip],
            recv_sem=kv_rsem.at[step, flip],
            device_id=((group + step) % GROUPS, member_of(zh, x, side)),
            device_id_type=MESH,
        )

    own_kv = pltpu.make_async_copy(send_kv.at[0, core], kv_ref.at[chip, core, 0], local_sem.at[0])
    own_kv.start()
    kv_copies = [kv_copy(s, f) for s in range(GROUPS) for f in range(2) if s or f]
    for copy in kv_copies:
        copy.start()

    for step in range(GROUPS):
        send_q[step] = q_ref[block_for(member, step)]

    def halves(ref, side):
        return ref.at[:, pl.ds(pl.multiple_of(side * HALF, HALF), HALF)]

    def do_peer():
        return pltpu.make_async_remote_copy(
            src_ref=halves(do_ref, other),
            dst_ref=do2_ref.at[core],
            send_sem=do_ssem,
            recv_sem=do_rsem,
            device_id=core_peer,
            device_id_type=MESH,
        )

    do_copy = do_peer()
    do_copy.start()
    own_do = pltpu.make_async_copy(halves(do_ref, core), do2_ref.at[core], local_sem.at[1])
    own_do.start()

    for copy in kv_copies:
        copy.wait()
    own_kv.wait()

    def send_region(index, src, dev):
        return pltpu.make_async_remote_copy(
            src_ref=src,
            dst_ref=src,
            send_sem=g_ssem.at[index],
            recv_sem=g_rsem.at[index],
            device_id=dev,
            device_id_type=MESH,
        )

    chip_z = (1 - zh) * 4 + x
    own_z = send_region(0, kv_ref.at[chip], z_peer)
    own_r = send_region(1, kv_ref.at[chip], r_peer)
    own_l = send_region(2, kv_ref.at[chip], l_peer)
    own_z.start()
    own_r.start()
    own_l.start()

    def q_copy(step, flip):
        side = core if flip == 0 else other
        return pltpu.make_async_remote_copy(
            src_ref=send_q.at[step, :, pl.ds(pl.multiple_of(side * HALF, HALF), HALF)],
            dst_ref=rq_ref.at[core, step],
            send_sem=q_ssem.at[step, flip],
            recv_sem=q_rsem.at[step, flip],
            device_id=((group + step) % GROUPS, member_of(zh, x, side)),
            device_id_type=MESH,
        )

    own_q = pltpu.make_async_copy(
        send_q.at[0, :, pl.ds(pl.multiple_of(core * HALF, HALF), HALF)], rq_ref.at[core, 0], local_sem.at[2]
    )
    own_q.start()
    q_copies = [q_copy(s, f) for s in range(GROUPS) for f in range(2) if s or f]
    for copy in q_copies:
        copy.start()

    def fill(row, carry):
        for step in range(GROUPS):
            b = block_for(row, step)
            table_ref[row * GROUPS + step] = order_ref[group, row * GROUPS + b]
        return carry

    lax.fori_loop(0, MEMBERS, fill, 0)
    for side in range(2):
        row = member_of(zh, x, side)
        for step in range(GROUPS):
            b = block_for(row, step)
            table_ref[128 + side * GROUPS + step] = order_ref[group, row * GROUPS + b]
            table_ref[144 + side * GROUPS + step] = b

    own_z.wait_recv()
    z_r = send_region(3, kv_ref.at[chip_z], r_peer)
    z_l = send_region(4, kv_ref.at[chip_z], l_peer)
    z_r.start()
    z_l.start()
    own_r.wait_recv()
    far_r = send_region(5, kv_ref.at[zh * 4 + left, 0], r_peer)
    far_r.start()
    own_l.wait_recv()
    far_l = send_region(6, kv_ref.at[zh * 4 + right, 1], l_peer)
    far_l.start()
    z_r.wait_recv()
    zfar_r = send_region(7, kv_ref.at[(1 - zh) * 4 + left, 0], r_peer)
    zfar_r.start()
    z_l.wait_recv()
    zfar_l = send_region(8, kv_ref.at[(1 - zh) * 4 + right, 1], l_peer)
    zfar_l.start()
    for copy in (far_r, far_l, zfar_r, zfar_l):
        copy.wait_recv()
    for copy in (own_z, own_r, own_l, z_r, z_l, far_r, far_l, zfar_r, zfar_l):
        copy.wait_send()
    for copy in q_copies:
        copy.wait()
    do_copy.wait()
    own_do.wait()
    own_q.wait()


def attend_kernel(
    table_ref, lengths_ref, order_ref, rq_ref, do_ref, kv_ref,
    attn_ref, dq_ref, dkv_ref,
    ks, acc, turned, sem,
):
    group = lax.axis_index("dp")

    def arrange(slot, carry):
        dst = pl.multiple_of(table_ref[slot] * BLOCK, BLOCK)
        pltpu.make_async_copy(kv_ref.at[slot], ks.at[pl.ds(dst, BLOCK)], sem).start()
        return carry

    lax.fori_loop(0, MEMBERS * GROUPS, arrange, 0)
    acc[...] = jnp.zeros_like(acc)
    pltpu.make_async_copy(ks, ks, sem).wait()

    def item(index, carry):
        p = table_ref[128 + index]
        out_row = pl.multiple_of((index // GROUPS) * ROWS + table_ref[144 + index] * BLOCK, BLOCK)
        in_row = pl.multiple_of(index * BLOCK, BLOCK)
        pos = p * BLOCK + lax.broadcasted_iota(jnp.int32, (BLOCK, CHUNK), 0)
        start = jnp.zeros((BLOCK, CHUNK), jnp.int32)
        first = jnp.int32(0)
        end = jnp.int32(0)
        for e in range(8):
            length = lengths_ref[group, e]
            end = end + length
            start = start + jnp.where(end <= pos, length, 0)
            first = first + jnp.where(end <= p * BLOCK, length, 0)
        low = first // CHUNK
        count = (p * BLOCK + BLOCK - 1) // CHUNK - low + 1
        base = pl.multiple_of(low * CHUNK, CHUNK)

        def run(n):
            width = n * CHUNK
            lanes = lax.broadcasted_iota(jnp.int32, (BLOCK, CHUNK), 1)
            parts = []
            for c in range(n):
                key = base + c * CHUNK + lanes
                parts.append(jnp.where((key >= start) & (key <= pos), 0.0, FILL).astype(jnp.float32))
            bias = jnp.concatenate(parts, axis=1) if n > 1 else parts[0]
            keys = pl.ds(base, width)
            for h in range(2):
                def heads(ref, row):
                    return jnp.concatenate(
                        [ref[pl.ds(row, BLOCK), pl.ds((h * PER_KEY + g) * HEAD, HEAD)] for g in range(PER_KEY)], axis=0
                    )

                q = heads(rq_ref, in_row)
                do = heads(do_ref, out_row)
                k = ks[keys, pl.ds(h * HEAD, HEAD)]
                v = ks[keys, pl.ds(KEYS_HALF + h * HEAD, HEAD)]
                s = lax.dot_general(q, k, (((1,), (1,)), ((), ())), preferred_element_type=jnp.float32)
                s = (s.reshape(PER_KEY, BLOCK, width) + bias[None]).reshape(PER_KEY * BLOCK, width)
                dp = lax.dot_general(do, v, (((1,), (1,)), ((), ())), preferred_element_type=jnp.float32)
                top = jnp.max(s, axis=1, keepdims=True)
                w = jnp.exp2((s - top) * (SCALE * LOG2E))
                total = jnp.sum(w, axis=1, keepdims=True)
                w_low = w.astype(jnp.bfloat16)
                inv = 1.0 / total
                out = lax.dot_general(w_low, v, (((1,), (0,)), ((), ())), preferred_element_type=jnp.float32)
                out = (out * inv).astype(jnp.bfloat16)
                do_wide = do.astype(jnp.float32)
                delta = jnp.sum(do_wide * out.astype(jnp.float32), axis=1, keepdims=True)
                ds = (w * (dp - delta)).astype(jnp.bfloat16)
                gq = lax.dot_general(ds, k, (((1,), (0,)), ((), ())), preferred_element_type=jnp.float32)
                gq = (gq * (inv * SCALE)).astype(jnp.bfloat16)
                qs = (q.astype(jnp.float32) * (inv * SCALE)).astype(jnp.bfloat16)
                dos = (do_wide * inv).astype(jnp.bfloat16)
                acc[h, 0, :, keys] += lax.dot_general(
                    qs, ds, (((0,), (0,)), ((), ())), preferred_element_type=jnp.float32
                )
                acc[h, 1, :, keys] += lax.dot_general(
                    dos, w_low, (((0,), (0,)), ((), ())), preferred_element_type=jnp.float32
                )
                for g in range(PER_KEY):
                    cols = pl.ds((h * PER_KEY + g) * HEAD, HEAD)
                    attn_ref[pl.ds(out_row, BLOCK), cols] = out[g * BLOCK:(g + 1) * BLOCK]
                    dq_ref[pl.ds(out_row, BLOCK), cols] = gq[g * BLOCK:(g + 1) * BLOCK]

        for n in range(1, MOST_CHUNKS + 1):
            pl.when(count == n)(functools.partial(run, n))
        return carry

    lax.fori_loop(0, 2 * GROUPS, item, 0)

    def turn(c, carry):
        keys = pl.ds(pl.multiple_of(c * CHUNK, CHUNK), CHUNK)
        for h in range(2):
            for which in range(2):
                turned[keys, pl.ds(which * KEYS_HALF + h * HEAD, HEAD)] = acc[h, which, :, keys].T.astype(jnp.bfloat16)
        return carry

    lax.fori_loop(0, GROUP_ROWS // CHUNK, turn, 0)

    def restore(slot, carry):
        src = pl.multiple_of(order_ref[group, slot] * BLOCK, BLOCK)
        pltpu.make_async_copy(turned.at[pl.ds(src, BLOCK)], dkv_ref.at[slot], sem).start()
        return carry

    lax.fori_loop(0, MEMBERS * GROUPS, restore, 0)
    pltpu.make_async_copy(dkv_ref, dkv_ref, sem).wait()


def scatter_kernel(
    attn2_ref, dq2_ref, u_ref,
    attn_ref, dq_ref, gk_ref, gv_ref,
    far_in, near_out, near_in, z_in, core_in, z_out, total, o_ssem, o_rsem, f_ssem, f_rsem, n_ssem, n_rsem, z_ssem, z_rsem, local_sem,
):
    group, zh, x, core = place()
    right, left, across = (x + 1) % 4, (x + 3) % 4, (x + 2) % 4
    other = 1 - core
    z_peer = (group, member_of(1 - zh, x, core))
    r_peer = (group, member_of(zh, right, core))
    l_peer = (group, member_of(zh, left, core))
    core_peer = (group, member_of(zh, x, other))
    barrier = pltpu.get_barrier_semaphore()
    for dev in (z_peer, r_peer, l_peer, core_peer):
        pl.semaphore_signal(barrier, inc=1, device_id=dev, device_id_type=MESH)
    pl.semaphore_wait(barrier, 4)

    def remote(src, dst, ssem, rsem, dev):
        return pltpu.make_async_remote_copy(
            src_ref=src, dst_ref=dst, send_sem=ssem, recv_sem=rsem, device_id=dev, device_id_type=MESH
        )

    planes = (1 - zh, zh)
    far = {}
    near = {}
    for p in range(2):
        for d, dev in ((0, r_peer), (1, l_peer)):
            far[p, d] = remote(
                u_ref.at[planes[p] * 4 + across, d], far_in.at[d, p], f_ssem.at[d, p], f_rsem.at[d, p], dev
            )
            far[p, d].start()
    for p in range(2):
        for d, dev, to in ((0, r_peer, right), (1, l_peer, left)):
            near[p, d, 1] = remote(
                u_ref.at[planes[p] * 4 + to, 1 - d], near_in.at[d, p, 1 - d], n_ssem.at[d, p, 1], n_rsem.at[d, p, 1], dev
            )
            near[p, d, 1].start()

    cols = pl.ds(pl.multiple_of(core * HALF, HALF), HALF)
    out_copies = []
    for i, (src, dst) in enumerate(((attn2_ref, attn_ref), (dq2_ref, dq_ref))):
        copy = remote(src.at[other], dst.at[:, cols], o_ssem.at[i], o_rsem.at[i], core_peer)
        copy.start()
        out_copies.append(copy)
        copy = pltpu.make_async_copy(src.at[core], dst.at[:, cols], local_sem.at[i])
        copy.start()
        out_copies.append(copy)

    for p in range(2):
        for d, dev, to in ((0, r_peer, right), (1, l_peer, left)):
            far[p, d].wait_recv()
            near_out[d, p] = (
                u_ref[planes[p] * 4 + to, d].astype(jnp.float32) + far_in[d, p].astype(jnp.float32)
            ).astype(jnp.bfloat16)
            near[p, d, 0] = remote(near_out.at[d, p], near_in.at[d, p, d], n_ssem.at[d, p, 0], n_rsem.at[d, p, 0], dev)
            near[p, d, 0].start()

    def summed(p):
        for d in range(2):
            for piece in range(2):
                near[p, d, piece].wait_recv()
        return (
            u_ref[planes[p] * 4 + x].astype(jnp.float32)
            + near_in[0, p].astype(jnp.float32)
            + near_in[1, p].astype(jnp.float32)
        )

    z_out[...] = summed(0).astype(jnp.bfloat16)
    z_copy = remote(z_out, z_in, z_ssem.at[0], z_rsem.at[0], z_peer)
    z_copy.start()
    mine = summed(1)
    z_copy.wait_recv()
    total[...] = (mine + z_in[...].astype(jnp.float32)).astype(jnp.bfloat16)
    core_copy = remote(total.at[other], core_in, z_ssem.at[1], z_rsem.at[1], core_peer)
    core_copy.start()
    here = pl.ds(pl.multiple_of(core * KEYS_HALF, KEYS_HALF), KEYS_HALF)
    there = pl.ds(pl.multiple_of(other * KEYS_HALF, KEYS_HALF), KEYS_HALF)
    gk_ref[:, here] = total[core, :, 0:KEYS_HALF]
    gv_ref[:, here] = total[core, :, KEYS_HALF:]
    core_copy.wait_recv()
    gk_ref[:, there] = core_in[:, 0:KEYS_HALF]
    gv_ref[:, there] = core_in[:, KEYS_HALF:]
    z_copy.wait_send()
    core_copy.wait_send()
    for copy in list(far.values()) + list(near.values()):
        copy.wait_send()
    for copy in out_copies:
        copy.wait()


VMEM = pl.BlockSpec(memory_space=pltpu.VMEM)
SMEM = pl.BlockSpec(memory_space=pltpu.SMEM)
ANY = pl.BlockSpec(memory_space=pl.ANY)


def on_device(queries, keys, values, output_gradient, doc_lengths, block_order, group_shift):
    low = jnp.bfloat16
    dma = pltpu.SemaphoreType.DMA
    rq, do2, kv, table = pl.pallas_call(
        gather_kernel,
        out_shape=(
            jax.ShapeDtypeStruct((2, GROUPS, BLOCK, HALF), low),
            jax.ShapeDtypeStruct((2, ROWS, HALF), low),
            jax.ShapeDtypeStruct((CHIPS, 2, GROUPS, BLOCK, 2 * KEYS_HALF), low),
            jax.ShapeDtypeStruct((256,), jnp.int32),
        ),
        in_specs=[VMEM, VMEM, VMEM, ANY, SMEM, SMEM],
        out_specs=(ANY, ANY, ANY, SMEM),
        scratch_shapes=[
            pltpu.VMEM((GROUPS, BLOCK, 2 * HALF), low),
            pltpu.VMEM((GROUPS, 2, BLOCK, 2 * KEYS_HALF), low),
            dma((GROUPS, 2)), dma((GROUPS, 2)),
            dma((GROUPS, 2)), dma((GROUPS, 2)),
            dma, dma,
            dma((9,)), dma((9,)),
            dma((3,)),
        ],
        compiler_params=pltpu.CompilerParams(collective_id=1, has_side_effects=True, vmem_limit_bytes=16 * MIB),
        name="move_and_gather",
    )(
        queries.reshape(GROUPS, BLOCK, 2 * HALF), keys.reshape(GROUPS, BLOCK, 2 * KEYS_HALF),
        values.reshape(GROUPS, BLOCK, 2 * KEYS_HALF), output_gradient, group_shift, block_order,
    )

    attn2, dq2, dkv = pl.pallas_call(
        attend_kernel,
        out_shape=(
            jax.ShapeDtypeStruct((2 * ROWS, HALF), low),
            jax.ShapeDtypeStruct((2 * ROWS, HALF), low),
            jax.ShapeDtypeStruct((MEMBERS * GROUPS, BLOCK, 2 * KEYS_HALF), low),
        ),
        in_specs=[SMEM, SMEM, SMEM, VMEM, VMEM, ANY],
        out_specs=(VMEM, VMEM, ANY),
        scratch_shapes=[
            pltpu.VMEM((GROUP_ROWS, 2 * KEYS_HALF), low),
            pltpu.VMEM((2, 2, HEAD, GROUP_ROWS), jnp.float32),
            pltpu.VMEM((GROUP_ROWS, 2 * KEYS_HALF), low),
            dma,
        ],
        compiler_params=pltpu.CompilerParams(vmem_limit_bytes=48 * MIB),
        name="attend",
    )(
        table, doc_lengths, block_order,
        rq.reshape(2 * ROWS, HALF), do2.reshape(2 * ROWS, HALF),
        kv.reshape(MEMBERS * GROUPS, BLOCK, 2 * KEYS_HALF),
    )

    return pl.pallas_call(
        scatter_kernel,
        out_shape=(
            jax.ShapeDtypeStruct((ROWS, 2 * HALF), low),
            jax.ShapeDtypeStruct((ROWS, 2 * HALF), low),
            jax.ShapeDtypeStruct((ROWS, 2 * KEYS_HALF), low),
            jax.ShapeDtypeStruct((ROWS, 2 * KEYS_HALF), low),
        ),
        in_specs=[ANY, ANY, VMEM],
        out_specs=(ANY, ANY, VMEM, VMEM),
        scratch_shapes=[
            pltpu.VMEM((2, 2, ROWS, 2 * KEYS_HALF), low),
            pltpu.VMEM((2, 2, ROWS, 2 * KEYS_HALF), low),
            pltpu.VMEM((2, 2, 2, ROWS, 2 * KEYS_HALF), low),
            pltpu.VMEM((2, ROWS, 2 * KEYS_HALF), low),
            pltpu.VMEM((ROWS, 2 * KEYS_HALF), low),
            pltpu.VMEM((2, ROWS, 2 * KEYS_HALF), low),
            pltpu.VMEM((2, ROWS, 2 * KEYS_HALF), low),
            dma((2,)), dma((2,)),
            dma((2, 2)), dma((2, 2)),
            dma((2, 2, 2)), dma((2, 2, 2)),
            dma((2,)), dma((2,)),
            dma((2,)),
        ],
        compiler_params=pltpu.CompilerParams(collective_id=2, has_side_effects=True, vmem_limit_bytes=32 * MIB),
        name="reduce_and_share",
    )(attn2.reshape(2, ROWS, HALF), dq2.reshape(2, ROWS, HALF), dkv.reshape(CHIPS, 2, ROWS, 2 * KEYS_HALF))


def solution(mesh):
    rows = P(("dp", "fsdp"), None)
    return jax.shard_map(
        on_device,
        mesh=mesh,
        in_specs=(rows, rows, rows, rows, P(), P(), P()),
        out_specs=(rows, rows, rows, rows),
        check_vma=False,
    )
```

```python
import functools
import math

import jax
import jax.numpy as jnp
from jax import lax
from jax.experimental import pallas as pl
from jax.experimental.pallas import tpu as pltpu
from jax.sharding import PartitionSpec as P

HEADS = 32
KEY_HEADS = 4
HEAD = 128
PER_KEY = 8
BLOCK = 16
ROWS = 128
GROUPS = 8
MEMBERS = 16
CHIPS = 8
GROUP_ROWS = 2048
HALF = HEADS * HEAD // 2
KEYS_HALF = KEY_HEADS * HEAD // 2
CHUNK = 128
MOST_CHUNKS = 9
DOCS = 8
TOGETHER = 2
SLOTS = GROUPS * MEMBERS
PIECES = 4
SCALE = 1.0 / math.sqrt(HEAD)
LOG2E = 1.4426950408889634
FILL = -1e30
MESH = pl.DeviceIdType.MESH
WHOLE = 56 << 20


def place():
    group = lax.axis_index("dp")
    member = lax.axis_index("fsdp")
    return group, member // 8, (member // 2) % 4, member % 2


def member_of(zh, x, core):
    return zh * 8 + x * 2 + core


def gather_kernel(
    q_ref, k_ref, v_ref, do_ref, shift_hbm, order_hbm, lengths_hbm,
    rq_ref, do2_ref, kv_ref, table_ref,
    shift_ref, order_ref, lengths_ref, counts, k_in, v_in, q_in, send_q, send_kv, own, q_land,
    in_sem, kv_ssem, kv_rsem, q_ssem, q_rsem, do_ssem, do_rsem, o_ssem, o_rsem, z_ssem, z_rsem, f_ssem, f_rsem, local_sem,
):
    group, zh, x, core = place()
    member = member_of(zh, x, core)
    chip = zh * 4 + x
    chip_z = (1 - zh) * 4 + x
    right, left = (x + 1) % 4, (x + 3) % 4
    other = 1 - core

    def peer(plane, col, side):
        return (group, member_of(plane, col, side))

    def remote(src, dst, ssem, rsem, dev):
        return pltpu.make_async_remote_copy(
            src_ref=src, dst_ref=dst, send_sem=ssem, recv_sem=rsem, device_id=dev, device_id_type=MESH
        )

    loads = [
        pltpu.make_async_copy(src, dst, in_sem.at[i])
        for i, (src, dst) in enumerate((
            (shift_hbm, shift_ref), (k_ref, k_in), (v_ref, v_in), (q_ref, q_in),
            (order_hbm, order_ref), (lengths_hbm, lengths_ref),
        ))
    ]
    for copy in loads:
        copy.start()

    barrier = pltpu.get_barrier_semaphore()
    greeted = 0
    for step in range(1, GROUPS):
        dev = ((group + GROUPS - step) % GROUPS, member)
        pl.semaphore_signal(barrier, inc=1, device_id=dev, device_id_type=MESH)
        greeted += 1
    around = [(1 - zh, x, 0), (1 - zh, x, 1)]
    for side in range(2):
        around += [(zh, right, side), (zh, left, side)]
    for spot in around + [(zh, x, other)]:
        pl.semaphore_signal(barrier, inc=1, device_id=peer(*spot), device_id_type=MESH)
        greeted += 1

    def block_for(row, step):
        found = jnp.int32(0)
        for b in range(GROUPS):
            found = jnp.maximum(found, jnp.where(shift_ref[b, row] == step, b, 0))
        return found

    loads[0].wait()
    blocks = [block_for(member, step) for step in range(GROUPS)]
    loads[1].wait()
    loads[2].wait()
    for step in range(GROUPS):
        for side in range(2):
            cols = slice(side * KEYS_HALF, (side + 1) * KEYS_HALF)
            send_kv[side, step, :, 0:KEYS_HALF] = k_in[blocks[step], :, cols]
            send_kv[side, step, :, KEYS_HALF:] = v_in[blocks[step], :, cols]

    pl.semaphore_wait(barrier, greeted)
    own_kv = pltpu.make_async_copy(send_kv.at[:, 0], own.at[:, 0], local_sem.at[0])
    own_kv.start()
    kv_copies = [
        remote(send_kv.at[:, s], own.at[:, s], kv_ssem.at[s], kv_rsem.at[s], ((group + s) % GROUPS, member))
        for s in range(1, GROUPS)
    ]
    for copy in kv_copies:
        copy.start()
    loads[3].wait()
    for step in range(GROUPS):
        send_q[step] = q_in[blocks[step]]

    def halves(ref, side):
        return ref.at[:, pl.ds(pl.multiple_of(side * HALF, HALF), HALF)]

    own_kv.wait()
    for copy in kv_copies:
        copy.wait_recv()
    def own_send(index, flip, dev_of):
        side = core if flip == 0 else other
        return remote(own.at[side], kv_ref.at[chip, core], o_ssem.at[index, flip], o_rsem.at[index, flip], dev_of(side))

    sends = []

    def go(copy):
        copy.start()
        sends.append(copy)
        return copy

    own_z = [go(own_send(0, f, lambda side: peer(1 - zh, x, side))) for f in range(2)]
    own_r = [go(own_send(1, f, lambda side: peer(zh, right, side))) for f in range(2)]
    own_l = [go(own_send(2, f, lambda side: peer(zh, left, side))) for f in range(2)]
    own_c = go(remote(own.at[other], kv_ref.at[chip, core], o_ssem.at[3, 0], o_rsem.at[3, 0], peer(zh, x, other)))
    own_here = pltpu.make_async_copy(own.at[core], kv_ref.at[chip, core], local_sem.at[1])
    own_here.start()

    def fill(row, carry):
        for step in range(GROUPS):
            b = block_for(row, step)
            table_ref[row * GROUPS + step] = order_ref[group, row * GROUPS + b]
        return carry

    loads[4].wait()
    loads[5].wait()
    lax.fori_loop(0, MEMBERS, fill, 0)
    for side in range(2):
        row = member_of(zh, x, side)
        for step in range(GROUPS):
            b = block_for(row, step)
            table_ref[128 + side * GROUPS + step] = order_ref[group, row * GROUPS + b]
            table_ref[144 + side * GROUPS + step] = b

    def count_chunks(index, carry):
        p = table_ref[128 + index] * BLOCK
        first = jnp.int32(0)
        end = jnp.int32(0)
        for e in range(DOCS):
            length = lengths_ref[group, e]
            end = end + length
            first = first + jnp.where(end <= p, length, 0)
        counts[index] = (p + BLOCK - 1) // CHUNK - first // CHUNK + 1
        return carry

    lax.fori_loop(0, 2 * GROUPS, count_chunks, 0)

    def rank_of(index, carry):
        mine = counts[index] * 16 + index
        rank = jnp.int32(0)
        for i in range(2 * GROUPS):
            rank = rank + jnp.where(counts[i] * 16 + i < mine, 1, 0)
        counts[16 + index] = rank
        return carry

    lax.fori_loop(0, 2 * GROUPS, rank_of, 0)

    def place_rank(rank, carry):
        found = jnp.int32(0)
        for i in range(2 * GROUPS):
            found = jnp.maximum(found, jnp.where(counts[16 + i] == rank, i, 0))
        table_ref[160 + rank] = found
        return carry

    lax.fori_loop(0, 2 * GROUPS, place_rank, 0)

    z_r, z_l = [None, None], [None, None]
    for f in range(2):
        own_z[f].wait_recv()
        src = kv_ref.at[chip_z, core if f == 0 else other]
        z_r[f] = go(remote(src, src, z_ssem.at[0, f], z_rsem.at[0, f], peer(zh, right, core)))
        z_l[f] = go(remote(src, src, z_ssem.at[1, f], z_rsem.at[1, f], peer(zh, left, core)))

    q_copies = [
        remote(send_q.at[s], q_land.at[s], q_ssem.at[s], q_rsem.at[s], ((group + s) % GROUPS, member))
        for s in range(1, GROUPS)
    ]
    for copy in q_copies[:3]:
        copy.start()
    do_copy = go(remote(halves(do_ref, other), do2_ref.at[core], do_ssem, do_rsem, peer(zh, x, other)))
    own_do = pltpu.make_async_copy(halves(do_ref, core), do2_ref.at[core], local_sem.at[2])
    own_do.start()

    own_r[0].wait_recv()
    src = kv_ref.at[zh * 4 + left, core]
    far_r = go(remote(src, src, f_ssem.at[0, 0], f_rsem.at[0, 0], peer(zh, right, core)))
    own_l[1].wait_recv()
    src = kv_ref.at[zh * 4 + right, other]
    far_l = go(remote(src, src, f_ssem.at[0, 1], f_rsem.at[0, 1], peer(zh, left, core)))
    for copy in q_copies[3:]:
        copy.start()
    own_r[1].wait_recv()
    own_l[0].wait_recv()
    z_r[0].wait_recv()
    src = kv_ref.at[(1 - zh) * 4 + left, core]
    zfar_r = go(remote(src, src, f_ssem.at[1, 0], f_rsem.at[1, 0], peer(zh, right, core)))
    z_l[1].wait_recv()
    src = kv_ref.at[(1 - zh) * 4 + right, other]
    zfar_l = go(remote(src, src, f_ssem.at[1, 1], f_rsem.at[1, 1], peer(zh, left, core)))

    def half_cols(ref, side):
        return ref.at[:, :, pl.ds(pl.multiple_of(side * HALF, HALF), HALF)]

    send_self = pltpu.make_async_copy(send_q.at[0], q_land.at[0], local_sem.at[3])
    send_self.start()
    send_self.wait()
    for copy in q_copies:
        copy.wait_recv()
        sends.append(copy)
    q_swap = go(remote(half_cols(q_land, other), rq_ref.at[core], q_ssem.at[0], q_rsem.at[0], peer(zh, x, other)))
    q_here = pltpu.make_async_copy(half_cols(q_land, core), rq_ref.at[core], local_sem.at[4])
    q_here.start()
    z_r[1].wait_recv()
    z_l[0].wait_recv()
    own_c.wait_recv()
    do_copy.wait_recv()
    for copy in (far_r, far_l, zfar_r, zfar_l):
        copy.wait_recv()
    q_swap.wait_recv()
    q_here.wait()
    own_do.wait()
    own_here.wait()
    for copy in kv_copies + sends:
        copy.wait_send()


def attend_kernel(
    table_ref, lengths_ref, order_ref, rq_hbm, do_hbm, kv_hbm,
    attn_hbm, dq_hbm, dkv_hbm,
    rq_ref, do_ref, kv_ref, attn_ref, dq_ref, dkv_ref, ks, acc, turned, in_sem, out_sem,
):
    group = lax.axis_index("dp")
    pieces = [pl.ds(i * SLOTS // PIECES, SLOTS // PIECES) for i in range(PIECES)]
    kv_loads = [
        pltpu.make_async_copy(kv_hbm.at[piece], kv_ref.at[piece], in_sem.at[2 + i]) for i, piece in enumerate(pieces)
    ]
    loads = [pltpu.make_async_copy(rq_hbm, rq_ref, in_sem.at[0]), pltpu.make_async_copy(do_hbm, do_ref, in_sem.at[1])]
    for copy in kv_loads + loads:
        copy.start()

    def arrange(slot, carry):
        dst = pl.multiple_of(table_ref[slot] * BLOCK, BLOCK)
        ks[pl.ds(dst, BLOCK), :] = kv_ref[slot]
        return carry

    acc[...] = jnp.zeros_like(acc)
    for i, copy in enumerate(kv_loads):
        copy.wait()
        lax.fori_loop(i * SLOTS // PIECES, (i + 1) * SLOTS // PIECES, arrange, 0, unroll=8)
    for copy in loads:
        copy.wait()

    def describe(index):
        p = table_ref[128 + index]
        out_row = pl.multiple_of((index // GROUPS) * ROWS + table_ref[144 + index] * BLOCK, BLOCK)
        in_row = pl.multiple_of(index * BLOCK, BLOCK)
        first = jnp.int32(0)
        end = jnp.int32(0)
        for e in range(DOCS):
            length = lengths_ref[group, e]
            end = end + length
            first = first + jnp.where(end <= p * BLOCK, length, 0)
        low = first // CHUNK
        count = (p * BLOCK + BLOCK - 1) // CHUNK - low + 1
        return p, in_row, out_row, low, count

    def tile(x, width):
        return (x.reshape(PER_KEY, BLOCK, width))

    def run(n, items):
        width = n * CHUNK
        lanes = lax.broadcasted_iota(jnp.int32, (BLOCK, CHUNK), 1)
        chains = []
        for p, in_row, out_row, low, count in items:
            pos = p * BLOCK + lax.broadcasted_iota(jnp.int32, (BLOCK, CHUNK), 0)
            start = jnp.zeros((BLOCK, CHUNK), jnp.int32)
            end = jnp.int32(0)
            for e in range(DOCS):
                length = lengths_ref[group, e]
                end = end + length
                start = start + jnp.where(end <= pos, length, 0)
            base = pl.multiple_of(jnp.minimum(low, GROUP_ROWS // CHUNK - n) * CHUNK, CHUNK)
            keys = pl.ds(base, width)
            parts = []
            for c in range(n):
                key = base + c * CHUNK + lanes
                parts.append(jnp.where((key >= start) & (key <= pos), 0.0, FILL).astype(jnp.float32))
            bias = jnp.concatenate(parts, axis=1) if n > 1 else parts[0]
            for h in range(2):
                def heads(ref, row):
                    return jnp.concatenate(
                        [ref[pl.ds(row, BLOCK), pl.ds((h * PER_KEY + g) * HEAD, HEAD)] for g in range(PER_KEY)], axis=0
                    )
                d = dict(h=h, keys=keys, bias=bias, out_row=out_row)
                d['q'] = heads(rq_ref, in_row)
                d['do'] = heads(do_ref, out_row)
                d['k'] = lambda d=d: ks[d['keys'], pl.ds(d['h'] * HEAD, HEAD)]
                d['v'] = lambda d=d: ks[d['keys'], pl.ds(KEYS_HALF + d['h'] * HEAD, HEAD)]
                chains.append(d)
        for d in chains:
            s = lax.dot_general(d['q'], d['k'](), (((1,), (1,)), ((), ())), preferred_element_type=jnp.float32)
            d['s'] = (tile(s, width) + d['bias'][None]).reshape(PER_KEY * BLOCK, width)
        for d in chains:
            d['top'] = jnp.max(d['s'], axis=1, keepdims=True)
        for d in chains:
            d['dp'] = lax.dot_general(d['do'], d['v'](), (((1,), (1,)), ((), ())), preferred_element_type=jnp.float32)
        for d in chains:
            w = jnp.exp2((d['s'] - d['top']) * (SCALE * LOG2E))
            d['w'] = w
            d['inv'] = 1.0 / jnp.sum(w, axis=1, keepdims=True)
            d['wl'] = w.astype(jnp.bfloat16)
        for d in chains:
            out = lax.dot_general(d['wl'], d['v'](), (((1,), (0,)), ((), ())), preferred_element_type=jnp.float32)
            d['out'] = (out * d['inv']).astype(jnp.bfloat16)
            dw = d['do'].astype(jnp.float32)
            d['delta'] = jnp.sum(dw * d['out'].astype(jnp.float32), axis=1, keepdims=True)
            d['qs'] = (d['q'].astype(jnp.float32) * (d['inv'] * SCALE)).astype(jnp.bfloat16)
            d['dos'] = (dw * d['inv']).astype(jnp.bfloat16)
        for d in chains:
            acc[d['h'], 1, :, d['keys']] += lax.dot_general(
                d['dos'], d['wl'], (((0,), (0,)), ((), ())), preferred_element_type=jnp.float32
            )
        for d in chains:
            d['ds'] = (d['w'] * (d['dp'] - d['delta'])).astype(jnp.bfloat16)
        for d in chains:
            gq = lax.dot_general(d['ds'], d['k'](), (((1,), (0,)), ((), ())), preferred_element_type=jnp.float32)
            d['gq'] = (gq * (d['inv'] * SCALE)).astype(jnp.bfloat16)
        for d in chains:
            acc[d['h'], 0, :, d['keys']] += lax.dot_general(
                d['qs'], d['ds'], (((0,), (0,)), ((), ())), preferred_element_type=jnp.float32
            )
        for d in chains:
            for g in range(PER_KEY):
                cols = pl.ds((d['h'] * PER_KEY + g) * HEAD, HEAD)
                attn_ref[pl.ds(d['out_row'], BLOCK), cols] = d['out'][g * BLOCK:(g + 1) * BLOCK]
                dq_ref[pl.ds(d['out_row'], BLOCK), cols] = d['gq'][g * BLOCK:(g + 1) * BLOCK]

    def item(step, carry):
        items = [describe(table_ref[160 + step * TOGETHER + i]) for i in range(TOGETHER)]
        count = items[0][4]
        for it in items[1:]:
            count = jnp.maximum(count, it[4])
        for n in range(1, MOST_CHUNKS + 1):
            pl.when(count == n)(functools.partial(run, n, items))
        return carry

    lax.fori_loop(0, 2 * GROUPS // TOGETHER, item, 0)
    stores = [
        pltpu.make_async_copy(attn_ref, attn_hbm, out_sem.at[0]), pltpu.make_async_copy(dq_ref, dq_hbm, out_sem.at[1])
    ]
    for copy in stores:
        copy.start()

    def turn(c, carry):
        keys = pl.ds(pl.multiple_of(c * CHUNK, CHUNK), CHUNK)
        for h in range(2):
            for which in range(2):
                turned[keys, pl.ds(which * KEYS_HALF + h * HEAD, HEAD)] = acc[h, which, :, keys].T.astype(jnp.bfloat16)
        return carry

    lax.fori_loop(0, GROUP_ROWS // CHUNK, turn, 0)

    def restore(slot, carry):
        src = pl.multiple_of(order_ref[group, slot] * BLOCK, BLOCK)
        dkv_ref[slot] = turned[pl.ds(src, BLOCK), :]
        return carry

    for i, piece in enumerate(pieces):
        lax.fori_loop(i * SLOTS // PIECES, (i + 1) * SLOTS // PIECES, restore, 0, unroll=8)
        copy = pltpu.make_async_copy(dkv_ref.at[piece], dkv_hbm.at[piece], out_sem.at[2 + i])
        copy.start()
        stores.append(copy)
    for copy in stores:
        copy.wait()


def scatter_kernel(
    attn2_ref, dq2_ref, u_hbm,
    attn_ref, dq_ref, grads_ref,
    u_ref, z0_in, far_out, far_in, cross_in, near_out, near_in, z1_out, z1_in, total,
    o_ssem, o_rsem, z_ssem, z_rsem, f_ssem, f_rsem, c_ssem, c_rsem, n_ssem, n_rsem, local_sem, u_sem,
):
    u_load = pltpu.make_async_copy(u_hbm, u_ref, u_sem)
    u_load.start()
    group, zh, x, core = place()
    right, left, across = (x + 1) % 4, (x + 3) % 4, (x + 2) % 4
    other = 1 - core
    z_peer = (group, member_of(1 - zh, x, core))
    r_peer = (group, member_of(zh, right, core))
    l_peer = (group, member_of(zh, left, core))
    core_peer = (group, member_of(zh, x, other))
    barrier = pltpu.get_barrier_semaphore()
    for dev in (z_peer, r_peer, l_peer, core_peer):
        pl.semaphore_signal(barrier, inc=1, device_id=dev, device_id_type=MESH)
    pl.semaphore_wait(barrier, 4)
    sends = []

    def go(src, dst, ssem, rsem, dev):
        copy = pltpu.make_async_remote_copy(
            src_ref=src, dst_ref=dst, send_sem=ssem, recv_sem=rsem, device_id=dev, device_id_type=MESH
        )
        copy.start()
        sends.append(copy)
        return copy

    def wide(value):
        return value.astype(jnp.float32)

    here, there = zh * 4, (1 - zh) * 4
    sides = ((0, r_peer, right), (1, l_peer, left))
    z0 = go(u_hbm.at[there + across], z0_in, z_ssem.at[0], z_rsem.at[0], z_peer)
    cross = [go(u_hbm.at[there + to], cross_in.at[d], c_ssem.at[d], c_rsem.at[d], dev) for d, dev, to in sides]
    outs = [
        go(src.at[other], dst, o_ssem.at[i], o_rsem.at[i], core_peer)
        for i, (src, dst) in enumerate(((attn2_ref, attn_ref), (dq2_ref, dq_ref)))
    ]
    u_load.wait()
    z0.wait_recv()
    far = []
    for d, dev, to in sides:
        far_out[d] = (wide(u_ref[here + across, d]) + wide(z0_in[d])).astype(jnp.bfloat16)
        far.append(go(far_out.at[d], far_in.at[d], f_ssem.at[d], f_rsem.at[d], dev))
    near = []
    for d, dev, to in sides:
        near.append(go(u_ref.at[here + to, 1 - d], near_in.at[d, 1 - d], n_ssem.at[d, 0], n_rsem.at[d, 0], dev))
    for copy in cross:
        copy.wait_recv()
    z1_out[...] = (wide(u_ref[there + x]) + wide(cross_in[0]) + wide(cross_in[1])).astype(jnp.bfloat16)
    z1 = go(z1_out, z1_in, z_ssem.at[1], z_rsem.at[1], z_peer)
    for d, dev, to in sides:
        far[d].wait_recv()
        near_out[d] = (wide(u_ref[here + to, d]) + wide(far_in[d])).astype(jnp.bfloat16)
        near.append(go(near_out.at[d], near_in.at[d, d], n_ssem.at[d, 1], n_rsem.at[d, 1], dev))
    z1.wait_recv()
    for copy in near:
        copy.wait_recv()
    total[...] = (
        wide(u_ref[here + x]) + wide(z1_in[...]) + wide(near_in[0]) + wide(near_in[1])
    ).astype(jnp.bfloat16)
    last = go(total.at[other], grads_ref.at[core], o_ssem.at[2], o_rsem.at[2], core_peer)
    kept = pltpu.make_async_copy(total.at[core], grads_ref.at[core], local_sem)
    kept.start()
    for copy in outs:
        copy.wait_recv()
    last.wait_recv()
    kept.wait()
    for copy in sends:
        copy.wait_send()


def finish_kernel(
    attn2_ref, dq2_ref, attn_in, dq_in, grads_in, attn_ref, dq_ref, gk_ref, gv_ref, wide, narrow, in_sem, out_sem,
):
    core = lax.axis_index("fsdp") % 2

    def cols(ref, side, width):
        return ref.at[:, pl.ds(pl.multiple_of(side * width, width), width)]

    groups = [
        (grads_in, narrow, [
            (narrow.at[side, :, pl.ds(which * KEYS_HALF, KEYS_HALF)], cols(dst, side, KEYS_HALF))
            for side in range(2) for which, dst in enumerate((gk_ref, gv_ref))
        ]),
        (attn2_ref.at[core], wide.at[0], [(wide.at[0], cols(attn_ref, core, HALF))]),
        (dq2_ref.at[core], wide.at[1], [(wide.at[1], cols(dq_ref, core, HALF))]),
        (attn_in, wide.at[2], [(wide.at[2], cols(attn_ref, 1 - core, HALF))]),
        (dq_in, wide.at[3], [(wide.at[3], cols(dq_ref, 1 - core, HALF))]),
    ]
    loads = [pltpu.make_async_copy(src, here, in_sem.at[i]) for i, (src, here, _) in enumerate(groups)]
    for copy in loads:
        copy.start()
    stores = []
    for copy, (_, _, pairs) in zip(loads, groups):
        copy.wait()
        for src, dst in pairs:
            out = pltpu.make_async_copy(src, dst, out_sem.at[len(stores)])
            out.start()
            stores.append(out)
    for copy in stores:
        copy.wait()


VMEM = pl.BlockSpec(memory_space=pltpu.VMEM)
SMEM = pl.BlockSpec(memory_space=pltpu.SMEM)
ANY = pl.BlockSpec(memory_space=pl.ANY)
HBM = pl.BlockSpec(memory_space=pltpu.HBM)


def on_device(queries, keys, values, output_gradient, doc_lengths, block_order, group_shift):
    low = jnp.bfloat16
    dma = pltpu.SemaphoreType.DMA
    rq, do2, kv, table = pl.pallas_call(
        gather_kernel,
        out_shape=(
            jax.ShapeDtypeStruct((2, GROUPS, BLOCK, HALF), low),
            jax.ShapeDtypeStruct((2, ROWS, HALF), low),
            jax.ShapeDtypeStruct((CHIPS, 2, GROUPS, BLOCK, 2 * KEYS_HALF), low),
            jax.ShapeDtypeStruct((256,), jnp.int32),
        ),
        in_specs=[HBM] * 7,
        out_specs=(ANY, ANY, ANY, SMEM),
        scratch_shapes=[
            pltpu.SMEM((GROUPS, MEMBERS), jnp.int32),
            pltpu.SMEM((GROUPS, MEMBERS * GROUPS), jnp.int32),
            pltpu.SMEM((GROUPS, DOCS), jnp.int32),
            pltpu.SMEM((32,), jnp.int32),
            pltpu.VMEM((GROUPS, BLOCK, 2 * KEYS_HALF), low),
            pltpu.VMEM((GROUPS, BLOCK, 2 * KEYS_HALF), low),
            pltpu.VMEM((GROUPS, BLOCK, 2 * HALF), low),
            pltpu.VMEM((GROUPS, BLOCK, 2 * HALF), low),
            pltpu.VMEM((2, GROUPS, BLOCK, 2 * KEYS_HALF), low),
            pltpu.VMEM((2, GROUPS, BLOCK, 2 * KEYS_HALF), low),
            pltpu.VMEM((GROUPS, BLOCK, 2 * HALF), low),
            dma((6,)),
            dma((GROUPS,)), dma((GROUPS,)),
            dma((GROUPS,)), dma((GROUPS,)),
            dma, dma,
            dma((4, 2)), dma((4, 2)),
            dma((2, 2)), dma((2, 2)),
            dma((2, 2)), dma((2, 2)),
            dma((5,)),
        ],
        compiler_params=pltpu.CompilerParams(collective_id=1, has_side_effects=True, vmem_limit_bytes=WHOLE),
        name="move_and_gather",
    )(
        queries.reshape(GROUPS, BLOCK, 2 * HALF), keys.reshape(GROUPS, BLOCK, 2 * KEYS_HALF),
        values.reshape(GROUPS, BLOCK, 2 * KEYS_HALF), output_gradient, group_shift.T, block_order, doc_lengths,
    )

    attn2, dq2, dkv = pl.pallas_call(
        attend_kernel,
        out_shape=(
            jax.ShapeDtypeStruct((2 * ROWS, HALF), low),
            jax.ShapeDtypeStruct((2 * ROWS, HALF), low),
            jax.ShapeDtypeStruct((SLOTS, BLOCK, 2 * KEYS_HALF), low),
        ),
        in_specs=[SMEM, SMEM, SMEM, ANY, ANY, ANY],
        out_specs=(ANY, ANY, ANY),
        scratch_shapes=[
            pltpu.VMEM((2 * ROWS, HALF), low), pltpu.VMEM((2 * ROWS, HALF), low),
            pltpu.VMEM((SLOTS, BLOCK, 2 * KEYS_HALF), low),
            pltpu.VMEM((2 * ROWS, HALF), low), pltpu.VMEM((2 * ROWS, HALF), low),
            pltpu.VMEM((SLOTS, BLOCK, 2 * KEYS_HALF), low),
            pltpu.VMEM((GROUP_ROWS, 2 * KEYS_HALF), low),
            pltpu.VMEM((2, 2, HEAD, GROUP_ROWS), jnp.float32),
            pltpu.VMEM((GROUP_ROWS, 2 * KEYS_HALF), low),
            dma((2 + PIECES,)), dma((2 + PIECES,)),
        ],
        compiler_params=pltpu.CompilerParams(vmem_limit_bytes=WHOLE),
        name="attend",
    )(
        table, doc_lengths, block_order,
        rq.reshape(2 * ROWS, HALF), do2.reshape(2 * ROWS, HALF),
        kv.reshape(SLOTS, BLOCK, 2 * KEYS_HALF),
    )
    attn2 = attn2.reshape(2, ROWS, HALF)
    dq2 = dq2.reshape(2, ROWS, HALF)

    region = (2, ROWS, 2 * KEYS_HALF)
    attn_in, dq_in, grads = pl.pallas_call(
        scatter_kernel,
        out_shape=(
            jax.ShapeDtypeStruct((ROWS, HALF), low),
            jax.ShapeDtypeStruct((ROWS, HALF), low),
            jax.ShapeDtypeStruct(region, low),
        ),
        in_specs=[ANY, ANY, ANY],
        out_specs=(ANY, ANY, ANY),
        scratch_shapes=[
            pltpu.VMEM((CHIPS,) + region, low),
            pltpu.VMEM(region, low),
            pltpu.VMEM(region, low), pltpu.VMEM(region, low),
            pltpu.VMEM((2,) + region, low),
            pltpu.VMEM(region, low), pltpu.VMEM((2,) + region, low),
            pltpu.VMEM(region, low), pltpu.VMEM(region, low),
            pltpu.VMEM(region, low),
            dma((3,)), dma((3,)),
            dma((2,)), dma((2,)),
            dma((2,)), dma((2,)),
            dma((2,)), dma((2,)),
            dma((2, 2)), dma((2, 2)),
            dma, dma,
        ],
        compiler_params=pltpu.CompilerParams(collective_id=2, has_side_effects=True, vmem_limit_bytes=WHOLE),
        name="reduce_and_share",
    )(attn2, dq2, dkv.reshape((CHIPS,) + region))

    return pl.pallas_call(
        finish_kernel,
        out_shape=(
            jax.ShapeDtypeStruct((ROWS, 2 * HALF), low),
            jax.ShapeDtypeStruct((ROWS, 2 * HALF), low),
            jax.ShapeDtypeStruct((ROWS, 2 * KEYS_HALF), low),
            jax.ShapeDtypeStruct((ROWS, 2 * KEYS_HALF), low),
        ),
        in_specs=[ANY] * 5,
        out_specs=(ANY,) * 4,
        scratch_shapes=[pltpu.VMEM((4, ROWS, HALF), low), pltpu.VMEM(region, low), dma((5,)), dma((8,))],
        compiler_params=pltpu.CompilerParams(vmem_limit_bytes=WHOLE),
        name="finish",
    )(attn2, dq2, attn_in, dq_in, grads)


def solution(mesh):
    rows = P(("dp", "fsdp"), None)
    return jax.shard_map(
        on_device,
        mesh=mesh,
        in_specs=(rows, rows, rows, rows, P(), P(), P()),
        out_specs=(rows, rows, rows, rows),
        check_vma=False,
    )
```

```python
import functools
import math

import jax
import jax.numpy as jnp
from jax import lax
from jax.experimental import pallas as pl
from jax.experimental.pallas import tpu as pltpu
from jax.sharding import PartitionSpec as P

HEADS = 32
KEY_HEADS = 4
HEAD = 128
PER_KEY = 8
BLOCK = 16
ROWS = 128
GROUPS = 8
MEMBERS = 16
CHIPS = 8
GROUP_ROWS = 2048
HALF = HEADS * HEAD // 2
KEYS_HALF = KEY_HEADS * HEAD // 2
CHUNK = 128
MOST_CHUNKS = 9
DOCS = 8
TOGETHER = 2
SLOTS = GROUPS * MEMBERS
PIECES = 4
SCALE = 1.0 / math.sqrt(HEAD)
LOG2E = 1.4426950408889634
FILL = -1e30
MESH = pl.DeviceIdType.MESH
WHOLE = 56 << 20


def place():
    group = lax.axis_index("dp")
    member = lax.axis_index("fsdp")
    return group, member // 8, (member // 2) % 4, member % 2


def member_of(zh, x, core):
    return zh * 8 + x * 2 + core


def gather_kernel(
    q_ref, k_ref, v_ref, do_ref, shift_hbm, order_hbm, lengths_hbm,
    rq_ref, do2_ref, kv_ref, table_ref,
    shift_ref, order_ref, lengths_ref, counts, k_in, v_in, q_in, send_q, send_kv, own,
    in_sem, kv_ssem, kv_rsem, q_ssem, q_rsem, do_ssem, do_rsem, o_ssem, o_rsem, c_sem, z_ssem, z_rsem, f_ssem, f_rsem, local_sem,
):
    group, zh, x, core = place()
    member = member_of(zh, x, core)
    chip = zh * 4 + x
    chip_z = (1 - zh) * 4 + x
    right, left = (x + 1) % 4, (x + 3) % 4
    other = 1 - core

    def peer(plane, col, side):
        return (group, member_of(plane, col, side))

    def remote(src, dst, ssem, rsem, dev):
        return pltpu.make_async_remote_copy(
            src_ref=src, dst_ref=dst, send_sem=ssem, recv_sem=rsem, device_id=dev, device_id_type=MESH
        )

    loads = [
        pltpu.make_async_copy(src, dst, in_sem.at[i])
        for i, (src, dst) in enumerate((
            (shift_hbm, shift_ref), (k_ref, k_in), (v_ref, v_in), (q_ref, q_in),
            (order_hbm, order_ref), (lengths_hbm, lengths_ref),
        ))
    ]
    for copy in loads:
        copy.start()

    def target(slot):
        return ((group // 4 + slot // 4) % 2) * 4 + (group % 4 + slot % 4) % 4

    def origin(slot):
        return ((group // 4 + slot // 4) % 2) * 4 + (group % 4 + 4 - slot % 4) % 4

    barrier = pltpu.get_barrier_semaphore()
    greeted = 0
    for slot in range(1, GROUPS):
        for side in range(2):
            dev = (origin(slot), member_of(zh, x, side))
            pl.semaphore_signal(barrier, inc=1, device_id=dev, device_id_type=MESH)
            greeted += 1
    around = [(1 - zh, x, 0), (1 - zh, x, 1)]
    for side in range(2):
        around += [(zh, right, side), (zh, left, side)]
    for spot in around + [(zh, x, other)]:
        pl.semaphore_signal(barrier, inc=1, device_id=peer(*spot), device_id_type=MESH)
        greeted += 1

    def block_for(row, step):
        found = jnp.int32(0)
        for b in range(GROUPS):
            found = jnp.maximum(found, jnp.where(shift_ref[b, row] == step, b, 0))
        return found

    loads[0].wait()
    blocks = [block_for(member, (target(slot) + GROUPS - group) % GROUPS) for slot in range(GROUPS)]
    loads[1].wait()
    loads[2].wait()
    for step in range(GROUPS):
        for side in range(2):
            cols = slice(side * KEYS_HALF, (side + 1) * KEYS_HALF)
            send_kv[side, step, :, 0:KEYS_HALF] = k_in[blocks[step], :, cols]
            send_kv[side, step, :, KEYS_HALF:] = v_in[blocks[step], :, cols]

    pl.semaphore_wait(barrier, greeted)
    own_kv = pltpu.make_async_copy(send_kv.at[:, 0], own.at[:, 0], local_sem.at[0])
    own_kv.start()
    kv_copies = [
        remote(send_kv.at[:, s], own.at[:, s], kv_ssem.at[s], kv_rsem.at[s], (target(s), member))
        for s in range(1, GROUPS)
    ]
    for copy in kv_copies:
        copy.start()
    loads[3].wait()
    for step in range(GROUPS):
        send_q[step] = q_in[blocks[step]]

    def halves(ref, side):
        return ref.at[:, pl.ds(pl.multiple_of(side * HALF, HALF), HALF)]

    def half_cols(ref, side):
        return ref.at[:, pl.ds(pl.multiple_of(side * HALF, HALF), HALF)]

    sends = []

    def go(copy):
        copy.start()
        sends.append(copy)
        return copy

    def q_send(slot, flip):
        side = core if flip == 0 else other
        return go(remote(
            half_cols(send_q.at[slot], side), rq_ref.at[core, slot],
            q_ssem.at[slot, flip], q_rsem.at[slot, flip], (target(slot), member_of(zh, x, side)),
        ))

    def own_send(index, flip, part, spot):
        side = core if flip == 0 else other
        some = pl.ds(part * 4, 4)
        return go(remote(
            own.at[side, some], kv_ref.at[chip, core, some],
            o_ssem.at[index, flip, part], o_rsem.at[index, flip, part], peer(*spot, side),
        ))

    own_kv.wait()
    own_z, own_r, own_l = {}, {}, {}
    arrived = 0
    for part in range(2):
        while arrived < (3, 7)[part]:
            kv_copies[arrived].wait_recv()
            arrived += 1
        for f in range(2):
            own_z[f, part] = own_send(0, f, part, (1 - zh, x))
            own_r[f, part] = own_send(1, f, part, (zh, right))
            own_l[f, part] = own_send(2, f, part, (zh, left))
    q_copies = [q_send(slot, flip) for slot in range(1, 4) for flip in range(2)]
    own_c = go(remote(own.at[other], kv_ref.at[chip, core], c_sem.at[0], c_sem.at[1], peer(zh, x, other)))
    own_here = pltpu.make_async_copy(own.at[core], kv_ref.at[chip, core], local_sem.at[1])
    own_here.start()
    q_copies.append(q_send(0, 1))
    q_here = pltpu.make_async_copy(half_cols(send_q.at[0], core), rq_ref.at[core, 0], local_sem.at[3])
    q_here.start()
    do_copy = go(remote(halves(do_ref, other), do2_ref.at[core], do_ssem, do_rsem, peer(zh, x, other)))
    own_do = pltpu.make_async_copy(halves(do_ref, core), do2_ref.at[core], local_sem.at[2])
    own_do.start()

    def came(copies, f):
        for part in range(2):
            copies[f, part].wait_recv()

    def fill(row, carry):
        for slot in range(GROUPS):
            b = block_for(row, (group + GROUPS - origin(slot)) % GROUPS)
            table_ref[row * GROUPS + slot] = order_ref[group, row * GROUPS + b]
        return carry

    loads[4].wait()
    loads[5].wait()
    lax.fori_loop(0, MEMBERS, fill, 0)
    for side in range(2):
        row = member_of(zh, x, side)
        for slot in range(GROUPS):
            b = block_for(row, (group + GROUPS - origin(slot)) % GROUPS)
            table_ref[128 + side * GROUPS + slot] = order_ref[group, row * GROUPS + b]
            table_ref[144 + side * GROUPS + slot] = b

    def count_chunks(index, carry):
        p = table_ref[128 + index] * BLOCK
        first = jnp.int32(0)
        end = jnp.int32(0)
        for e in range(DOCS):
            length = lengths_ref[group, e]
            end = end + length
            first = first + jnp.where(end <= p, length, 0)
        counts[index] = (p + BLOCK - 1) // CHUNK - first // CHUNK + 1
        return carry

    lax.fori_loop(0, 2 * GROUPS, count_chunks, 0)

    def rank_of(index, carry):
        mine = counts[index] * 16 + index
        rank = jnp.int32(0)
        for i in range(2 * GROUPS):
            rank = rank + jnp.where(counts[i] * 16 + i < mine, 1, 0)
        counts[16 + index] = rank
        return carry

    lax.fori_loop(0, 2 * GROUPS, rank_of, 0)

    def place_rank(rank, carry):
        found = jnp.int32(0)
        for i in range(2 * GROUPS):
            found = jnp.maximum(found, jnp.where(counts[16 + i] == rank, i, 0))
        table_ref[160 + rank] = found
        return carry

    lax.fori_loop(0, 2 * GROUPS, place_rank, 0)

    z_r, z_l = [None, None], [None, None]
    for f in range(2):
        came(own_z, f)
        src = kv_ref.at[chip_z, core if f == 0 else other]
        z_r[f] = go(remote(src, src, z_ssem.at[0, f], z_rsem.at[0, f], peer(zh, right, core)))
        z_l[f] = go(remote(src, src, z_ssem.at[1, f], z_rsem.at[1, f], peer(zh, left, core)))

    q_copies += [q_send(slot, flip) for slot in range(4, GROUPS) for flip in range(2)]
    came(own_r, 0)
    src = kv_ref.at[zh * 4 + left, core]
    far_r = go(remote(src, src, f_ssem.at[0, 0], f_rsem.at[0, 0], peer(zh, right, core)))
    came(own_l, 1)
    src = kv_ref.at[zh * 4 + right, other]
    far_l = go(remote(src, src, f_ssem.at[0, 1], f_rsem.at[0, 1], peer(zh, left, core)))
    came(own_r, 1)
    came(own_l, 0)
    z_r[0].wait_recv()
    src = kv_ref.at[(1 - zh) * 4 + left, core]
    zfar_r = go(remote(src, src, f_ssem.at[1, 0], f_rsem.at[1, 0], peer(zh, right, core)))
    z_l[1].wait_recv()
    src = kv_ref.at[(1 - zh) * 4 + right, other]
    zfar_l = go(remote(src, src, f_ssem.at[1, 1], f_rsem.at[1, 1], peer(zh, left, core)))

    z_r[1].wait_recv()
    z_l[0].wait_recv()
    own_c.wait_recv()
    do_copy.wait_recv()
    for copy in (far_r, far_l, zfar_r, zfar_l):
        copy.wait_recv()
    for copy in q_copies:
        copy.wait_recv()
    q_here.wait()
    own_do.wait()
    own_here.wait()
    for copy in kv_copies + sends:
        copy.wait_send()


def attend_kernel(
    table_ref, lengths_ref, order_ref, rq_hbm, do_hbm, kv_hbm,
    attn_hbm, dq_hbm, dkv_hbm,
    rq_ref, do_ref, kv_ref, attn_ref, dq_ref, dkv_ref, ks, acc, turned, in_sem, out_sem,
):
    group = lax.axis_index("dp")
    pieces = [pl.ds(i * SLOTS // PIECES, SLOTS // PIECES) for i in range(PIECES)]
    kv_loads = [
        pltpu.make_async_copy(kv_hbm.at[piece], kv_ref.at[piece], in_sem.at[2 + i]) for i, piece in enumerate(pieces)
    ]
    loads = [pltpu.make_async_copy(rq_hbm, rq_ref, in_sem.at[0]), pltpu.make_async_copy(do_hbm, do_ref, in_sem.at[1])]
    for copy in kv_loads + loads:
        copy.start()

    def arrange(slot, carry):
        dst = pl.multiple_of(table_ref[slot] * BLOCK, BLOCK)
        ks[pl.ds(dst, BLOCK), :] = kv_ref[slot]
        return carry

    acc[...] = jnp.zeros_like(acc)
    for i, copy in enumerate(kv_loads):
        copy.wait()
        lax.fori_loop(i * SLOTS // PIECES, (i + 1) * SLOTS // PIECES, arrange, 0, unroll=8)
    for copy in loads:
        copy.wait()

    def describe(index):
        p = table_ref[128 + index]
        out_row = pl.multiple_of((index // GROUPS) * ROWS + table_ref[144 + index] * BLOCK, BLOCK)
        in_row = pl.multiple_of(index * BLOCK, BLOCK)
        first = jnp.int32(0)
        end = jnp.int32(0)
        for e in range(DOCS):
            length = lengths_ref[group, e]
            end = end + length
            first = first + jnp.where(end <= p * BLOCK, length, 0)
        low = first // CHUNK
        count = (p * BLOCK + BLOCK - 1) // CHUNK - low + 1
        return p, in_row, out_row, low, count

    def tile(x, width):
        return (x.reshape(PER_KEY, BLOCK, width))

    def run(n, items):
        width = n * CHUNK
        lanes = lax.broadcasted_iota(jnp.int32, (BLOCK, CHUNK), 1)
        chains = []
        for p, in_row, out_row, low, count in items:
            pos = p * BLOCK + lax.broadcasted_iota(jnp.int32, (BLOCK, CHUNK), 0)
            start = jnp.zeros((BLOCK, CHUNK), jnp.int32)
            end = jnp.int32(0)
            for e in range(DOCS):
                length = lengths_ref[group, e]
                end = end + length
                start = start + jnp.where(end <= pos, length, 0)
            base = pl.multiple_of(jnp.minimum(low, GROUP_ROWS // CHUNK - n) * CHUNK, CHUNK)
            keys = pl.ds(base, width)
            parts = []
            for c in range(n):
                key = base + c * CHUNK + lanes
                parts.append(jnp.where((key >= start) & (key <= pos), 0.0, FILL).astype(jnp.float32))
            bias = jnp.concatenate(parts, axis=1) if n > 1 else parts[0]
            for h in range(2):
                def heads(ref, row):
                    return jnp.concatenate(
                        [ref[pl.ds(row, BLOCK), pl.ds((h * PER_KEY + g) * HEAD, HEAD)] for g in range(PER_KEY)], axis=0
                    )
                d = dict(h=h, keys=keys, bias=bias, out_row=out_row)
                d['q'] = heads(rq_ref, in_row)
                d['do'] = heads(do_ref, out_row)
                d['k'] = lambda d=d: ks[d['keys'], pl.ds(d['h'] * HEAD, HEAD)]
                d['v'] = lambda d=d: ks[d['keys'], pl.ds(KEYS_HALF + d['h'] * HEAD, HEAD)]
                chains.append(d)
        for d in chains:
            s = lax.dot_general(d['q'], d['k'](), (((1,), (1,)), ((), ())), preferred_element_type=jnp.float32)
            d['s'] = (tile(s, width) + d['bias'][None]).reshape(PER_KEY * BLOCK, width)
        for d in chains:
            d['top'] = jnp.max(d['s'], axis=1, keepdims=True)
        for d in chains:
            d['dp'] = lax.dot_general(d['do'], d['v'](), (((1,), (1,)), ((), ())), preferred_element_type=jnp.float32)
        for d in chains:
            w = jnp.exp2((d['s'] - d['top']) * (SCALE * LOG2E))
            d['w'] = w
            d['inv'] = 1.0 / jnp.sum(w, axis=1, keepdims=True)
            d['wl'] = w.astype(jnp.bfloat16)
        for d in chains:
            out = lax.dot_general(d['wl'], d['v'](), (((1,), (0,)), ((), ())), preferred_element_type=jnp.float32)
            d['out'] = (out * d['inv']).astype(jnp.bfloat16)
            dw = d['do'].astype(jnp.float32)
            d['delta'] = jnp.sum(dw * d['out'].astype(jnp.float32), axis=1, keepdims=True)
            d['qs'] = (d['q'].astype(jnp.float32) * (d['inv'] * SCALE)).astype(jnp.bfloat16)
            d['dos'] = (dw * d['inv']).astype(jnp.bfloat16)
        for d in chains:
            acc[d['h'], 1, :, d['keys']] += lax.dot_general(
                d['dos'], d['wl'], (((0,), (0,)), ((), ())), preferred_element_type=jnp.float32
            )
        for d in chains:
            d['ds'] = (d['w'] * (d['dp'] - d['delta'])).astype(jnp.bfloat16)
        for d in chains:
            gq = lax.dot_general(d['ds'], d['k'](), (((1,), (0,)), ((), ())), preferred_element_type=jnp.float32)
            d['gq'] = (gq * (d['inv'] * SCALE)).astype(jnp.bfloat16)
        for d in chains:
            acc[d['h'], 0, :, d['keys']] += lax.dot_general(
                d['qs'], d['ds'], (((0,), (0,)), ((), ())), preferred_element_type=jnp.float32
            )
        for d in chains:
            for g in range(PER_KEY):
                cols = pl.ds((d['h'] * PER_KEY + g) * HEAD, HEAD)
                attn_ref[pl.ds(d['out_row'], BLOCK), cols] = d['out'][g * BLOCK:(g + 1) * BLOCK]
                dq_ref[pl.ds(d['out_row'], BLOCK), cols] = d['gq'][g * BLOCK:(g + 1) * BLOCK]

    def item(step, carry):
        items = [describe(table_ref[160 + step * TOGETHER + i]) for i in range(TOGETHER)]
        count = items[0][4]
        for it in items[1:]:
            count = jnp.maximum(count, it[4])
        for n in range(1, MOST_CHUNKS + 1):
            pl.when(count == n)(functools.partial(run, n, items))
        return carry

    lax.fori_loop(0, 2 * GROUPS // TOGETHER, item, 0)
    stores = [
        pltpu.make_async_copy(attn_ref, attn_hbm, out_sem.at[0]), pltpu.make_async_copy(dq_ref, dq_hbm, out_sem.at[1])
    ]
    for copy in stores:
        copy.start()

    def turn(c, carry):
        keys = pl.ds(pl.multiple_of(c * CHUNK, CHUNK), CHUNK)
        for h in range(2):
            for which in range(2):
                turned[keys, pl.ds(which * KEYS_HALF + h * HEAD, HEAD)] = acc[h, which, :, keys].T.astype(jnp.bfloat16)
        return carry

    lax.fori_loop(0, GROUP_ROWS // CHUNK, turn, 0)

    def restore(slot, carry):
        src = pl.multiple_of(order_ref[group, slot] * BLOCK, BLOCK)
        dkv_ref[slot] = turned[pl.ds(src, BLOCK), :]
        return carry

    for i, piece in enumerate(pieces):
        lax.fori_loop(i * SLOTS // PIECES, (i + 1) * SLOTS // PIECES, restore, 0, unroll=8)
        copy = pltpu.make_async_copy(dkv_ref.at[piece], dkv_hbm.at[piece], out_sem.at[2 + i])
        copy.start()
        stores.append(copy)
    for copy in stores:
        copy.wait()


def scatter_kernel(
    attn2_ref, dq2_ref, u_hbm,
    attn_ref, dq_ref, grads_ref,
    u_ref, z0_in, far_out, far_in, cross_in, near_out, near_in, z1_out, z1_in, total,
    o_ssem, o_rsem, z_ssem, z_rsem, f_ssem, f_rsem, c_ssem, c_rsem, n_ssem, n_rsem, local_sem, u_sem,
):
    u_load = pltpu.make_async_copy(u_hbm, u_ref, u_sem)
    u_load.start()
    group, zh, x, core = place()
    right, left, across = (x + 1) % 4, (x + 3) % 4, (x + 2) % 4
    other = 1 - core
    z_peer = (group, member_of(1 - zh, x, core))
    r_peer = (group, member_of(zh, right, core))
    l_peer = (group, member_of(zh, left, core))
    core_peer = (group, member_of(zh, x, other))
    barrier = pltpu.get_barrier_semaphore()
    for dev in (z_peer, r_peer, l_peer, core_peer):
        pl.semaphore_signal(barrier, inc=1, device_id=dev, device_id_type=MESH)
    pl.semaphore_wait(barrier, 4)
    sends = []

    def go(src, dst, ssem, rsem, dev):
        copy = pltpu.make_async_remote_copy(
            src_ref=src, dst_ref=dst, send_sem=ssem, recv_sem=rsem, device_id=dev, device_id_type=MESH
        )
        copy.start()
        sends.append(copy)
        return copy

    def wide(value):
        return value.astype(jnp.float32)

    here, there = zh * 4, (1 - zh) * 4
    sides = ((0, r_peer, right), (1, l_peer, left))
    z0 = go(u_hbm.at[there + across], z0_in, z_ssem.at[0], z_rsem.at[0], z_peer)
    cross = [go(u_hbm.at[there + to], cross_in.at[d], c_ssem.at[d], c_rsem.at[d], dev) for d, dev, to in sides]
    outs = [
        go(src.at[other], dst, o_ssem.at[i], o_rsem.at[i], core_peer)
        for i, (src, dst) in enumerate(((attn2_ref, attn_ref), (dq2_ref, dq_ref)))
    ]
    u_load.wait()
    z0.wait_recv()
    far = []
    for d, dev, to in sides:
        far_out[d] = (wide(u_ref[here + across, d]) + wide(z0_in[d])).astype(jnp.bfloat16)
        far.append(go(far_out.at[d], far_in.at[d], f_ssem.at[d], f_rsem.at[d], dev))
    near = []
    for d, dev, to in sides:
        near.append(go(u_ref.at[here + to, 1 - d], near_in.at[d, 1 - d], n_ssem.at[d, 0], n_rsem.at[d, 0], dev))
    for copy in cross:
        copy.wait_recv()
    z1_out[...] = (wide(u_ref[there + x]) + wide(cross_in[0]) + wide(cross_in[1])).astype(jnp.bfloat16)
    z1 = go(z1_out, z1_in, z_ssem.at[1], z_rsem.at[1], z_peer)
    for d, dev, to in sides:
        far[d].wait_recv()
        near_out[d] = (wide(u_ref[here + to, d]) + wide(far_in[d])).astype(jnp.bfloat16)
        near.append(go(near_out.at[d], near_in.at[d, d], n_ssem.at[d, 1], n_rsem.at[d, 1], dev))
    z1.wait_recv()
    for copy in near:
        copy.wait_recv()
    total[...] = (
        wide(u_ref[here + x]) + wide(z1_in[...]) + wide(near_in[0]) + wide(near_in[1])
    ).astype(jnp.bfloat16)
    last = go(total.at[other], grads_ref.at[core], o_ssem.at[2], o_rsem.at[2], core_peer)
    kept = pltpu.make_async_copy(total.at[core], grads_ref.at[core], local_sem)
    kept.start()
    for copy in outs:
        copy.wait_recv()
    last.wait_recv()
    kept.wait()
    for copy in sends:
        copy.wait_send()


def finish_kernel(
    attn2_ref, dq2_ref, attn_in, dq_in, grads_in, attn_ref, dq_ref, gk_ref, gv_ref, wide, narrow, in_sem, out_sem,
):
    core = lax.axis_index("fsdp") % 2

    def cols(ref, side, width):
        return ref.at[:, pl.ds(pl.multiple_of(side * width, width), width)]

    groups = [
        (grads_in, narrow, [
            (narrow.at[side, :, pl.ds(which * KEYS_HALF, KEYS_HALF)], cols(dst, side, KEYS_HALF))
            for side in range(2) for which, dst in enumerate((gk_ref, gv_ref))
        ]),
        (attn2_ref.at[core], wide.at[0], [(wide.at[0], cols(attn_ref, core, HALF))]),
        (dq2_ref.at[core], wide.at[1], [(wide.at[1], cols(dq_ref, core, HALF))]),
        (attn_in, wide.at[2], [(wide.at[2], cols(attn_ref, 1 - core, HALF))]),
        (dq_in, wide.at[3], [(wide.at[3], cols(dq_ref, 1 - core, HALF))]),
    ]
    loads = [pltpu.make_async_copy(src, here, in_sem.at[i]) for i, (src, here, _) in enumerate(groups)]
    for copy in loads:
        copy.start()
    stores = []
    for copy, (_, _, pairs) in zip(loads, groups):
        copy.wait()
        for src, dst in pairs:
            out = pltpu.make_async_copy(src, dst, out_sem.at[len(stores)])
            out.start()
            stores.append(out)
    for copy in stores:
        copy.wait()


VMEM = pl.BlockSpec(memory_space=pltpu.VMEM)
SMEM = pl.BlockSpec(memory_space=pltpu.SMEM)
ANY = pl.BlockSpec(memory_space=pl.ANY)
HBM = pl.BlockSpec(memory_space=pltpu.HBM)


def on_device(queries, keys, values, output_gradient, doc_lengths, block_order, group_shift):
    low = jnp.bfloat16
    dma = pltpu.SemaphoreType.DMA
    rq, do2, kv, table = pl.pallas_call(
        gather_kernel,
        out_shape=(
            jax.ShapeDtypeStruct((2, GROUPS, BLOCK, HALF), low),
            jax.ShapeDtypeStruct((2, ROWS, HALF), low),
            jax.ShapeDtypeStruct((CHIPS, 2, GROUPS, BLOCK, 2 * KEYS_HALF), low),
            jax.ShapeDtypeStruct((256,), jnp.int32),
        ),
        in_specs=[HBM] * 7,
        out_specs=(ANY, ANY, ANY, SMEM),
        scratch_shapes=[
            pltpu.SMEM((GROUPS, MEMBERS), jnp.int32),
            pltpu.SMEM((GROUPS, MEMBERS * GROUPS), jnp.int32),
            pltpu.SMEM((GROUPS, DOCS), jnp.int32),
            pltpu.SMEM((32,), jnp.int32),
            pltpu.VMEM((GROUPS, BLOCK, 2 * KEYS_HALF), low),
            pltpu.VMEM((GROUPS, BLOCK, 2 * KEYS_HALF), low),
            pltpu.VMEM((GROUPS, BLOCK, 2 * HALF), low),
            pltpu.VMEM((GROUPS, BLOCK, 2 * HALF), low),
            pltpu.VMEM((2, GROUPS, BLOCK, 2 * KEYS_HALF), low),
            pltpu.VMEM((2, GROUPS, BLOCK, 2 * KEYS_HALF), low),
            dma((6,)),
            dma((GROUPS,)), dma((GROUPS,)),
            dma((GROUPS, 2)), dma((GROUPS, 2)),
            dma, dma,
            dma((3, 2, 2)), dma((3, 2, 2)), dma((2,)),
            dma((2, 2)), dma((2, 2)),
            dma((2, 2)), dma((2, 2)),
            dma((5,)),
        ],
        compiler_params=pltpu.CompilerParams(collective_id=1, has_side_effects=True, vmem_limit_bytes=WHOLE),
        name="move_and_gather",
    )(
        queries.reshape(GROUPS, BLOCK, 2 * HALF), keys.reshape(GROUPS, BLOCK, 2 * KEYS_HALF),
        values.reshape(GROUPS, BLOCK, 2 * KEYS_HALF), output_gradient, group_shift.T, block_order, doc_lengths,
    )

    attn2, dq2, dkv = pl.pallas_call(
        attend_kernel,
        out_shape=(
            jax.ShapeDtypeStruct((2 * ROWS, HALF), low),
            jax.ShapeDtypeStruct((2 * ROWS, HALF), low),
            jax.ShapeDtypeStruct((SLOTS, BLOCK, 2 * KEYS_HALF), low),
        ),
        in_specs=[SMEM, SMEM, SMEM, ANY, ANY, ANY],
        out_specs=(ANY, ANY, ANY),
        scratch_shapes=[
            pltpu.VMEM((2 * ROWS, HALF), low), pltpu.VMEM((2 * ROWS, HALF), low),
            pltpu.VMEM((SLOTS, BLOCK, 2 * KEYS_HALF), low),
            pltpu.VMEM((2 * ROWS, HALF), low), pltpu.VMEM((2 * ROWS, HALF), low),
            pltpu.VMEM((SLOTS, BLOCK, 2 * KEYS_HALF), low),
            pltpu.VMEM((GROUP_ROWS, 2 * KEYS_HALF), low),
            pltpu.VMEM((2, 2, HEAD, GROUP_ROWS), jnp.float32),
            pltpu.VMEM((GROUP_ROWS, 2 * KEYS_HALF), low),
            dma((2 + PIECES,)), dma((2 + PIECES,)),
        ],
        compiler_params=pltpu.CompilerParams(vmem_limit_bytes=WHOLE),
        name="attend",
    )(
        table, doc_lengths, block_order,
        rq.reshape(2 * ROWS, HALF), do2.reshape(2 * ROWS, HALF),
        kv.reshape(SLOTS, BLOCK, 2 * KEYS_HALF),
    )
    attn2 = attn2.reshape(2, ROWS, HALF)
    dq2 = dq2.reshape(2, ROWS, HALF)

    region = (2, ROWS, 2 * KEYS_HALF)
    attn_in, dq_in, grads = pl.pallas_call(
        scatter_kernel,
        out_shape=(
            jax.ShapeDtypeStruct((ROWS, HALF), low),
            jax.ShapeDtypeStruct((ROWS, HALF), low),
            jax.ShapeDtypeStruct(region, low),
        ),
        in_specs=[ANY, ANY, ANY],
        out_specs=(ANY, ANY, ANY),
        scratch_shapes=[
            pltpu.VMEM((CHIPS,) + region, low),
            pltpu.VMEM(region, low),
            pltpu.VMEM(region, low), pltpu.VMEM(region, low),
            pltpu.VMEM((2,) + region, low),
            pltpu.VMEM(region, low), pltpu.VMEM((2,) + region, low),
            pltpu.VMEM(region, low), pltpu.VMEM(region, low),
            pltpu.VMEM(region, low),
            dma((3,)), dma((3,)),
            dma((2,)), dma((2,)),
            dma((2,)), dma((2,)),
            dma((2,)), dma((2,)),
            dma((2, 2)), dma((2, 2)),
            dma, dma,
        ],
        compiler_params=pltpu.CompilerParams(collective_id=2, has_side_effects=True, vmem_limit_bytes=WHOLE),
        name="reduce_and_share",
    )(attn2, dq2, dkv.reshape((CHIPS,) + region))

    return pl.pallas_call(
        finish_kernel,
        out_shape=(
            jax.ShapeDtypeStruct((ROWS, 2 * HALF), low),
            jax.ShapeDtypeStruct((ROWS, 2 * HALF), low),
            jax.ShapeDtypeStruct((ROWS, 2 * KEYS_HALF), low),
            jax.ShapeDtypeStruct((ROWS, 2 * KEYS_HALF), low),
        ),
        in_specs=[ANY] * 5,
        out_specs=(ANY,) * 4,
        scratch_shapes=[pltpu.VMEM((4, ROWS, HALF), low), pltpu.VMEM(region, low), dma((5,)), dma((8,))],
        compiler_params=pltpu.CompilerParams(vmem_limit_bytes=WHOLE),
        name="finish",
    )(attn2, dq2, attn_in, dq_in, grads)


def solution(mesh):
    rows = P(("dp", "fsdp"), None)
    return jax.shard_map(
        on_device,
        mesh=mesh,
        in_specs=(rows, rows, rows, rows, P(), P(), P()),
        out_specs=(rows, rows, rows, rows),
        check_vma=False,
    )
```

```python
import functools
import math

import jax
import jax.numpy as jnp
from jax import lax
from jax.experimental import pallas as pl
from jax.experimental.pallas import tpu as pltpu
from jax.sharding import PartitionSpec as P

HEADS = 32
KEY_HEADS = 4
HEAD = 128
PER_KEY = 8
BLOCK = 16
ROWS = 128
GROUPS = 8
MEMBERS = 16
CHIPS = 8
GROUP_ROWS = 2048
HALF = HEADS * HEAD // 2
KEYS_HALF = KEY_HEADS * HEAD // 2
CHUNK = 128
MOST_CHUNKS = 9
DOCS = 8
TOGETHER = 2
SLOTS = GROUPS * MEMBERS
PIECES = 4
SCALE = 1.0 / math.sqrt(HEAD)
LOG2E = 1.4426950408889634
FILL = -1e30
MESH = pl.DeviceIdType.MESH
WHOLE = 56 << 20


def place():
    group = lax.axis_index("dp")
    member = lax.axis_index("fsdp")
    return group, member // 8, (member // 2) % 4, member % 2


def member_of(zh, x, core):
    return zh * 8 + x * 2 + core


def gather_kernel(
    q_ref, k_ref, v_ref, do_ref, shift_hbm, order_hbm, lengths_hbm,
    rq_ref, do2_ref, kv_ref, table_ref,
    shift_ref, order_ref, lengths_ref, counts, k_in, v_in, q_in, send_q, send_kv, own,
    in_sem, kv_ssem, kv_rsem, q_ssem, q_rsem, do_ssem, do_rsem, o_ssem, o_rsem, c_sem, z_ssem, z_rsem, f_ssem, f_rsem, local_sem,
):
    group, zh, x, core = place()
    member = member_of(zh, x, core)
    chip = zh * 4 + x
    chip_z = (1 - zh) * 4 + x
    right, left = (x + 1) % 4, (x + 3) % 4
    other = 1 - core

    def peer(plane, col, side):
        return (group, member_of(plane, col, side))

    def remote(src, dst, ssem, rsem, dev):
        return pltpu.make_async_remote_copy(
            src_ref=src, dst_ref=dst, send_sem=ssem, recv_sem=rsem, device_id=dev, device_id_type=MESH
        )

    loads = [
        pltpu.make_async_copy(src, dst, in_sem.at[i])
        for i, (src, dst) in enumerate((
            (shift_hbm, shift_ref), (k_ref, k_in), (v_ref, v_in), (q_ref, q_in),
            (order_hbm, order_ref), (lengths_hbm, lengths_ref),
        ))
    ]
    for copy in loads:
        copy.start()

    def target(slot):
        return ((group // 4 + slot // 4) % 2) * 4 + (group % 4 + slot % 4) % 4

    def origin(slot):
        return ((group // 4 + slot // 4) % 2) * 4 + (group % 4 + 4 - slot % 4) % 4

    barrier = pltpu.get_barrier_semaphore()
    greeted = 0
    for slot in range(1, GROUPS):
        for side in range(2):
            dev = (origin(slot), member_of(zh, x, side))
            pl.semaphore_signal(barrier, inc=1, device_id=dev, device_id_type=MESH)
            greeted += 1
    around = [(1 - zh, x, 0), (1 - zh, x, 1)]
    for side in range(2):
        around += [(zh, right, side), (zh, left, side)]
    for spot in around + [(zh, x, other)]:
        pl.semaphore_signal(barrier, inc=1, device_id=peer(*spot), device_id_type=MESH)
        greeted += 1

    def block_for(row, step):
        found = jnp.int32(0)
        for b in range(GROUPS):
            found = jnp.maximum(found, jnp.where(shift_ref[b, row] == step, b, 0))
        return found

    loads[0].wait()
    blocks = [block_for(member, (target(slot) + GROUPS - group) % GROUPS) for slot in range(GROUPS)]
    loads[1].wait()
    loads[2].wait()
    for step in range(GROUPS):
        for side in range(2):
            cols = slice(side * KEYS_HALF, (side + 1) * KEYS_HALF)
            send_kv[side, step, :, 0:KEYS_HALF] = k_in[blocks[step], :, cols]
            send_kv[side, step, :, KEYS_HALF:] = v_in[blocks[step], :, cols]

    pl.semaphore_wait(barrier, greeted)
    own_kv = pltpu.make_async_copy(send_kv.at[:, 0], own.at[:, 0], local_sem.at[0])
    own_kv.start()
    kv_copies = [
        remote(send_kv.at[:, s], own.at[:, s], kv_ssem.at[s], kv_rsem.at[s], (target(s), member))
        for s in range(1, GROUPS)
    ]
    for copy in kv_copies:
        copy.start()
    loads[3].wait()
    for step in range(GROUPS):
        send_q[step] = q_in[blocks[step]]

    def halves(ref, side):
        return ref.at[:, pl.ds(pl.multiple_of(side * HALF, HALF), HALF)]

    def half_cols(ref, side):
        return ref.at[:, pl.ds(pl.multiple_of(side * HALF, HALF), HALF)]

    sends = []

    def go(copy):
        copy.start()
        sends.append(copy)
        return copy

    def q_send(slot, flip):
        side = core if flip == 0 else other
        return go(remote(
            half_cols(send_q.at[slot], side), rq_ref.at[core, slot],
            q_ssem.at[slot, flip], q_rsem.at[slot, flip], (target(slot), member_of(zh, x, side)),
        ))

    def own_send(index, flip, part, spot):
        side = core if flip == 0 else other
        some = pl.ds(part * 4, 4)
        return go(remote(
            own.at[side, some], kv_ref.at[chip, core, some],
            o_ssem.at[index, flip, part], o_rsem.at[index, flip, part], peer(*spot, side),
        ))

    own_kv.wait()
    own_z, own_r, own_l = {}, {}, {}
    arrived = 0
    for part in range(2):
        while arrived < (3, 7)[part]:
            kv_copies[arrived].wait_recv()
            arrived += 1
        for f in range(2):
            own_z[f, part] = own_send(0, f, part, (1 - zh, x))
            own_r[f, part] = own_send(1, f, part, (zh, right))
            own_l[f, part] = own_send(2, f, part, (zh, left))
    q_copies = [q_send(slot, flip) for slot in range(1, 4) for flip in range(2)]
    own_c = go(remote(own.at[other], kv_ref.at[chip, core], c_sem.at[0], c_sem.at[1], peer(zh, x, other)))
    own_here = pltpu.make_async_copy(own.at[core], kv_ref.at[chip, core], local_sem.at[1])
    own_here.start()
    q_copies.append(q_send(0, 1))
    q_here = pltpu.make_async_copy(half_cols(send_q.at[0], core), rq_ref.at[core, 0], local_sem.at[3])
    q_here.start()
    do_copy = go(remote(halves(do_ref, other), do2_ref.at[core], do_ssem, do_rsem, peer(zh, x, other)))
    own_do = pltpu.make_async_copy(halves(do_ref, core), do2_ref.at[core], local_sem.at[2])
    own_do.start()

    def came(copies, f):
        for part in range(2):
            copies[f, part].wait_recv()

    def fill(row, carry):
        for slot in range(GROUPS):
            b = block_for(row, (group + GROUPS - origin(slot)) % GROUPS)
            table_ref[row * GROUPS + slot] = order_ref[group, row * GROUPS + b]
        return carry

    loads[4].wait()
    loads[5].wait()
    lax.fori_loop(0, MEMBERS, fill, 0)
    for side in range(2):
        row = member_of(zh, x, side)
        for slot in range(GROUPS):
            b = block_for(row, (group + GROUPS - origin(slot)) % GROUPS)
            table_ref[128 + side * GROUPS + slot] = order_ref[group, row * GROUPS + b]
            table_ref[144 + side * GROUPS + slot] = b

    def count_chunks(index, carry):
        p = table_ref[128 + index] * BLOCK
        first = jnp.int32(0)
        end = jnp.int32(0)
        for e in range(DOCS):
            length = lengths_ref[group, e]
            end = end + length
            first = first + jnp.where(end <= p, length, 0)
        counts[index] = (p + BLOCK - 1) // CHUNK - first // CHUNK + 1
        return carry

    lax.fori_loop(0, 2 * GROUPS, count_chunks, 0)

    def rank_of(index, carry):
        mine = counts[index] * 16 + index
        rank = jnp.int32(0)
        for i in range(2 * GROUPS):
            rank = rank + jnp.where(counts[i] * 16 + i < mine, 1, 0)
        counts[16 + index] = rank
        return carry

    lax.fori_loop(0, 2 * GROUPS, rank_of, 0)

    def place_rank(rank, carry):
        found = jnp.int32(0)
        for i in range(2 * GROUPS):
            found = jnp.maximum(found, jnp.where(counts[16 + i] == rank, i, 0))
        table_ref[160 + rank] = found
        return carry

    lax.fori_loop(0, 2 * GROUPS, place_rank, 0)

    z_r, z_l = [None, None], [None, None]
    for f in range(2):
        came(own_z, f)
        src = kv_ref.at[chip_z, core if f == 0 else other]
        z_r[f] = go(remote(src, src, z_ssem.at[0, f], z_rsem.at[0, f], peer(zh, right, core)))
        z_l[f] = go(remote(src, src, z_ssem.at[1, f], z_rsem.at[1, f], peer(zh, left, core)))

    q_copies += [q_send(slot, flip) for slot in range(4, GROUPS) for flip in range(2)]
    came(own_r, 0)
    src = kv_ref.at[zh * 4 + left, core]
    far_r = go(remote(src, src, f_ssem.at[0, 0], f_rsem.at[0, 0], peer(zh, right, core)))
    came(own_l, 1)
    src = kv_ref.at[zh * 4 + right, other]
    far_l = go(remote(src, src, f_ssem.at[0, 1], f_rsem.at[0, 1], peer(zh, left, core)))
    came(own_r, 1)
    came(own_l, 0)
    z_r[0].wait_recv()
    src = kv_ref.at[(1 - zh) * 4 + left, core]
    zfar_r = go(remote(src, src, f_ssem.at[1, 0], f_rsem.at[1, 0], peer(zh, right, core)))
    z_l[1].wait_recv()
    src = kv_ref.at[(1 - zh) * 4 + right, other]
    zfar_l = go(remote(src, src, f_ssem.at[1, 1], f_rsem.at[1, 1], peer(zh, left, core)))

    z_r[1].wait_recv()
    z_l[0].wait_recv()
    own_c.wait_recv()
    do_copy.wait_recv()
    for copy in (far_r, far_l, zfar_r, zfar_l):
        copy.wait_recv()
    for copy in q_copies:
        copy.wait_recv()
    q_here.wait()
    own_do.wait()
    own_here.wait()
    for copy in kv_copies + sends:
        copy.wait_send()


def attend_kernel(
    table_ref, lengths_ref, order_ref, rq_hbm, do_hbm, kv_hbm,
    attn_full, dq_full, attn_send, dq_send, dkv_hbm,
    rq_ref, do_ref, kv_ref, attn_ref, dq_ref, dkv_ref, ks, acc, turned, in_sem, out_sem,
):
    group = lax.axis_index("dp")
    pieces = [pl.ds(i * SLOTS // PIECES, SLOTS // PIECES) for i in range(PIECES)]
    kv_loads = [
        pltpu.make_async_copy(kv_hbm.at[piece], kv_ref.at[piece], in_sem.at[2 + i]) for i, piece in enumerate(pieces)
    ]
    loads = [pltpu.make_async_copy(rq_hbm, rq_ref, in_sem.at[0]), pltpu.make_async_copy(do_hbm, do_ref, in_sem.at[1])]
    for copy in kv_loads + loads:
        copy.start()

    def arrange(slot, carry):
        dst = pl.multiple_of(table_ref[slot] * BLOCK, BLOCK)
        ks[pl.ds(dst, BLOCK), :] = kv_ref[slot]
        return carry

    acc[...] = jnp.zeros_like(acc)
    for i, copy in enumerate(kv_loads):
        copy.wait()
        lax.fori_loop(i * SLOTS // PIECES, (i + 1) * SLOTS // PIECES, arrange, 0, unroll=8)
    for copy in loads:
        copy.wait()

    def describe(index):
        p = table_ref[128 + index]
        out_row = pl.multiple_of((index // GROUPS) * ROWS + table_ref[144 + index] * BLOCK, BLOCK)
        in_row = pl.multiple_of(index * BLOCK, BLOCK)
        first = jnp.int32(0)
        end = jnp.int32(0)
        for e in range(DOCS):
            length = lengths_ref[group, e]
            end = end + length
            first = first + jnp.where(end <= p * BLOCK, length, 0)
        low = first // CHUNK
        count = (p * BLOCK + BLOCK - 1) // CHUNK - low + 1
        return p, in_row, out_row, low, count

    def tile(x, width):
        return (x.reshape(PER_KEY, BLOCK, width))

    def run(n, items):
        width = n * CHUNK
        lanes = lax.broadcasted_iota(jnp.int32, (BLOCK, CHUNK), 1)
        chains = []
        for p, in_row, out_row, low, count in items:
            pos = p * BLOCK + lax.broadcasted_iota(jnp.int32, (BLOCK, CHUNK), 0)
            start = jnp.zeros((BLOCK, CHUNK), jnp.int32)
            end = jnp.int32(0)
            for e in range(DOCS):
                length = lengths_ref[group, e]
                end = end + length
                start = start + jnp.where(end <= pos, length, 0)
            base = pl.multiple_of(jnp.minimum(low, GROUP_ROWS // CHUNK - n) * CHUNK, CHUNK)
            keys = pl.ds(base, width)
            parts = []
            for c in range(n):
                key = base + c * CHUNK + lanes
                parts.append(jnp.where((key >= start) & (key <= pos), 0.0, FILL).astype(jnp.float32))
            bias = jnp.concatenate(parts, axis=1) if n > 1 else parts[0]
            for h in range(2):
                def heads(ref, row):
                    return jnp.concatenate(
                        [ref[pl.ds(row, BLOCK), pl.ds((h * PER_KEY + g) * HEAD, HEAD)] for g in range(PER_KEY)], axis=0
                    )
                d = dict(h=h, keys=keys, bias=bias, out_row=out_row)
                d['q'] = heads(rq_ref, in_row)
                d['do'] = heads(do_ref, out_row)
                d['k'] = lambda d=d: ks[d['keys'], pl.ds(d['h'] * HEAD, HEAD)]
                d['v'] = lambda d=d: ks[d['keys'], pl.ds(KEYS_HALF + d['h'] * HEAD, HEAD)]
                chains.append(d)
        for d in chains:
            s = lax.dot_general(d['q'], d['k'](), (((1,), (1,)), ((), ())), preferred_element_type=jnp.float32)
            d['s'] = (tile(s, width) + d['bias'][None]).reshape(PER_KEY * BLOCK, width)
        for d in chains:
            d['top'] = jnp.max(d['s'], axis=1, keepdims=True)
        for d in chains:
            d['dp'] = lax.dot_general(d['do'], d['v'](), (((1,), (1,)), ((), ())), preferred_element_type=jnp.float32)
        for d in chains:
            w = jnp.exp2((d['s'] - d['top']) * (SCALE * LOG2E))
            d['w'] = w
            d['inv'] = 1.0 / jnp.sum(w, axis=1, keepdims=True)
            d['wl'] = w.astype(jnp.bfloat16)
        for d in chains:
            out = lax.dot_general(d['wl'], d['v'](), (((1,), (0,)), ((), ())), preferred_element_type=jnp.float32)
            d['out'] = (out * d['inv']).astype(jnp.bfloat16)
            dw = d['do'].astype(jnp.float32)
            d['delta'] = jnp.sum(dw * d['out'].astype(jnp.float32), axis=1, keepdims=True)
            d['qs'] = (d['q'].astype(jnp.float32) * (d['inv'] * SCALE)).astype(jnp.bfloat16)
            d['dos'] = (dw * d['inv']).astype(jnp.bfloat16)
        for d in chains:
            acc[d['h'], 1, :, d['keys']] += lax.dot_general(
                d['dos'], d['wl'], (((0,), (0,)), ((), ())), preferred_element_type=jnp.float32
            )
        for d in chains:
            d['ds'] = (d['w'] * (d['dp'] - d['delta'])).astype(jnp.bfloat16)
        for d in chains:
            gq = lax.dot_general(d['ds'], d['k'](), (((1,), (0,)), ((), ())), preferred_element_type=jnp.float32)
            d['gq'] = (gq * (d['inv'] * SCALE)).astype(jnp.bfloat16)
        for d in chains:
            acc[d['h'], 0, :, d['keys']] += lax.dot_general(
                d['qs'], d['ds'], (((0,), (0,)), ((), ())), preferred_element_type=jnp.float32
            )
        for d in chains:
            for g in range(PER_KEY):
                cols = pl.ds((d['h'] * PER_KEY + g) * HEAD, HEAD)
                attn_ref[pl.ds(d['out_row'], BLOCK), cols] = d['out'][g * BLOCK:(g + 1) * BLOCK]
                dq_ref[pl.ds(d['out_row'], BLOCK), cols] = d['gq'][g * BLOCK:(g + 1) * BLOCK]

    def item(step, carry):
        items = [describe(table_ref[160 + step * TOGETHER + i]) for i in range(TOGETHER)]
        count = items[0][4]
        for it in items[1:]:
            count = jnp.maximum(count, it[4])
        for n in range(1, MOST_CHUNKS + 1):
            pl.when(count == n)(functools.partial(run, n, items))
        return carry

    lax.fori_loop(0, 2 * GROUPS // TOGETHER, item, 0)
    core = lax.axis_index("fsdp") % 2
    cols = pl.ds(pl.multiple_of(core * HALF, HALF), HALF)
    kept = pl.ds(pl.multiple_of(core * ROWS, ROWS), ROWS)
    sent = pl.ds(pl.multiple_of((1 - core) * ROWS, ROWS), ROWS)
    stores = [
        pltpu.make_async_copy(attn_ref.at[sent], attn_send, out_sem.at[0]),
        pltpu.make_async_copy(dq_ref.at[sent], dq_send, out_sem.at[1]),
        pltpu.make_async_copy(attn_ref.at[kept], attn_full.at[:, cols], out_sem.at[2]),
        pltpu.make_async_copy(dq_ref.at[kept], dq_full.at[:, cols], out_sem.at[3]),
    ]
    for copy in stores:
        copy.start()

    def turn(c, carry):
        keys = pl.ds(pl.multiple_of(c * CHUNK, CHUNK), CHUNK)
        for h in range(2):
            for which in range(2):
                turned[keys, pl.ds(which * KEYS_HALF + h * HEAD, HEAD)] = acc[h, which, :, keys].T.astype(jnp.bfloat16)
        return carry

    lax.fori_loop(0, GROUP_ROWS // CHUNK, turn, 0)

    def restore(slot, carry):
        src = pl.multiple_of(order_ref[group, slot] * BLOCK, BLOCK)
        dkv_ref[slot] = turned[pl.ds(src, BLOCK), :]
        return carry

    for i, piece in enumerate(pieces):
        lax.fori_loop(i * SLOTS // PIECES, (i + 1) * SLOTS // PIECES, restore, 0, unroll=8)
        copy = pltpu.make_async_copy(dkv_ref.at[piece], dkv_hbm.at[piece], out_sem.at[4 + i])
        copy.start()
        stores.append(copy)
    for copy in stores:
        copy.wait()


def scatter_kernel(
    attn_send, dq_send, u_hbm,
    attn_ref, dq_ref, grads_ref,
    u_ref, z0_in, far_out, far_in, cross_in, near_out, near_in, z1_out, z1_in, total,
    o_ssem, o_rsem, z_ssem, z_rsem, f_ssem, f_rsem, c_ssem, c_rsem, n_ssem, n_rsem, local_sem, u_sem,
):
    u_load = pltpu.make_async_copy(u_hbm, u_ref, u_sem)
    u_load.start()
    group, zh, x, core = place()
    right, left, across = (x + 1) % 4, (x + 3) % 4, (x + 2) % 4
    other = 1 - core
    z_peer = (group, member_of(1 - zh, x, core))
    r_peer = (group, member_of(zh, right, core))
    l_peer = (group, member_of(zh, left, core))
    core_peer = (group, member_of(zh, x, other))
    barrier = pltpu.get_barrier_semaphore()
    for dev in (z_peer, r_peer, l_peer, core_peer):
        pl.semaphore_signal(barrier, inc=1, device_id=dev, device_id_type=MESH)
    pl.semaphore_wait(barrier, 4)
    sends = []

    def go(src, dst, ssem, rsem, dev):
        copy = pltpu.make_async_remote_copy(
            src_ref=src, dst_ref=dst, send_sem=ssem, recv_sem=rsem, device_id=dev, device_id_type=MESH
        )
        copy.start()
        sends.append(copy)
        return copy

    def wide(value):
        return value.astype(jnp.float32)

    here, there = zh * 4, (1 - zh) * 4
    sides = ((0, r_peer, right), (1, l_peer, left))
    parts = [pl.ds(i * ROWS // 2, ROWS // 2) for i in range(2)]
    z0 = {
        (q, d): go(
            u_hbm.at[there + across, d, parts[q]], z0_in.at[d, parts[q]], z_ssem.at[2 * q + d], z_rsem.at[2 * q + d], z_peer
        )
        for q in range(2) for d in range(2)
    }
    cross = [go(u_hbm.at[there + to], cross_in.at[d], c_ssem.at[d], c_rsem.at[d], dev) for d, dev, to in sides]
    outs = [
        go(src, dst, o_ssem.at[i], o_rsem.at[i], core_peer)
        for i, (src, dst) in enumerate(((attn_send, attn_ref), (dq_send, dq_ref)))
    ]
    u_load.wait()
    far, near = {}, []

    def send_far(q):
        for d, dev, to in sides:
            z0[q, d].wait_recv()
            far_out[d, parts[q]] = (wide(u_ref[here + across, d, parts[q]]) + wide(z0_in[d, parts[q]])).astype(jnp.bfloat16)
            far[q, d] = go(far_out.at[d, parts[q]], far_in.at[d, parts[q]], f_ssem.at[d, q], f_rsem.at[d, q], dev)

    send_far(0)
    for d, dev, to in sides:
        near.append(go(u_ref.at[here + to, 1 - d], near_in.at[d, 1 - d], n_ssem.at[d, 0], n_rsem.at[d, 0], dev))
    for copy in cross:
        copy.wait_recv()
    z1_out[...] = (wide(u_ref[there + x]) + wide(cross_in[0]) + wide(cross_in[1])).astype(jnp.bfloat16)
    z1 = go(z1_out, z1_in, z_ssem.at[4], z_rsem.at[4], z_peer)
    send_far(1)
    for q in range(2):
        for d, dev, to in sides:
            far[q, d].wait_recv()
            near_out[d, parts[q]] = (wide(u_ref[here + to, d, parts[q]]) + wide(far_in[d, parts[q]])).astype(jnp.bfloat16)
            near.append(go(
                near_out.at[d, parts[q]], near_in.at[d, d, parts[q]], n_ssem.at[d, 1 + q], n_rsem.at[d, 1 + q], dev
            ))
    z1.wait_recv()
    for copy in near:
        copy.wait_recv()
    total[...] = (
        wide(u_ref[here + x]) + wide(z1_in[...]) + wide(near_in[0]) + wide(near_in[1])
    ).astype(jnp.bfloat16)
    last = go(total.at[other], grads_ref.at[core], o_ssem.at[2], o_rsem.at[2], core_peer)
    kept = pltpu.make_async_copy(total.at[core], grads_ref.at[core], local_sem)
    kept.start()
    for copy in outs:
        copy.wait_recv()
    last.wait_recv()
    kept.wait()
    for copy in sends:
        copy.wait_send()


def finish_kernel(
    attn_full, dq_full, attn_in, dq_in, grads_in, attn_ref, dq_ref, gk_ref, gv_ref, wide, narrow, in_sem, out_sem,
):
    core = lax.axis_index("fsdp") % 2

    def cols(ref, side, width):
        return ref.at[:, pl.ds(pl.multiple_of(side * width, width), width)]

    groups = [
        (grads_in, narrow, [
            (narrow.at[side, :, pl.ds(which * KEYS_HALF, KEYS_HALF)], cols(dst, side, KEYS_HALF))
            for side in range(2) for which, dst in enumerate((gk_ref, gv_ref))
        ]),
        (attn_in, wide.at[0], [(wide.at[0], cols(attn_ref, 1 - core, HALF))]),
        (dq_in, wide.at[1], [(wide.at[1], cols(dq_ref, 1 - core, HALF))]),
    ]
    loads = [pltpu.make_async_copy(src, here, in_sem.at[i]) for i, (src, here, _) in enumerate(groups)]
    for copy in loads:
        copy.start()
    stores = []
    for copy, (_, _, pairs) in zip(loads, groups):
        copy.wait()
        for src, dst in pairs:
            out = pltpu.make_async_copy(src, dst, out_sem.at[len(stores)])
            out.start()
            stores.append(out)
    for copy in stores:
        copy.wait()


VMEM = pl.BlockSpec(memory_space=pltpu.VMEM)
SMEM = pl.BlockSpec(memory_space=pltpu.SMEM)
ANY = pl.BlockSpec(memory_space=pl.ANY)
HBM = pl.BlockSpec(memory_space=pltpu.HBM)


def on_device(queries, keys, values, output_gradient, doc_lengths, block_order, group_shift):
    low = jnp.bfloat16
    dma = pltpu.SemaphoreType.DMA
    rq, do2, kv, table = pl.pallas_call(
        gather_kernel,
        out_shape=(
            jax.ShapeDtypeStruct((2, GROUPS, BLOCK, HALF), low),
            jax.ShapeDtypeStruct((2, ROWS, HALF), low),
            jax.ShapeDtypeStruct((CHIPS, 2, GROUPS, BLOCK, 2 * KEYS_HALF), low),
            jax.ShapeDtypeStruct((256,), jnp.int32),
        ),
        in_specs=[HBM] * 7,
        out_specs=(ANY, ANY, ANY, SMEM),
        scratch_shapes=[
            pltpu.SMEM((GROUPS, MEMBERS), jnp.int32),
            pltpu.SMEM((GROUPS, MEMBERS * GROUPS), jnp.int32),
            pltpu.SMEM((GROUPS, DOCS), jnp.int32),
            pltpu.SMEM((32,), jnp.int32),
            pltpu.VMEM((GROUPS, BLOCK, 2 * KEYS_HALF), low),
            pltpu.VMEM((GROUPS, BLOCK, 2 * KEYS_HALF), low),
            pltpu.VMEM((GROUPS, BLOCK, 2 * HALF), low),
            pltpu.VMEM((GROUPS, BLOCK, 2 * HALF), low),
            pltpu.VMEM((2, GROUPS, BLOCK, 2 * KEYS_HALF), low),
            pltpu.VMEM((2, GROUPS, BLOCK, 2 * KEYS_HALF), low),
            dma((6,)),
            dma((GROUPS,)), dma((GROUPS,)),
            dma((GROUPS, 2)), dma((GROUPS, 2)),
            dma, dma,
            dma((3, 2, 2)), dma((3, 2, 2)), dma((2,)),
            dma((2, 2)), dma((2, 2)),
            dma((2, 2)), dma((2, 2)),
            dma((5,)),
        ],
        compiler_params=pltpu.CompilerParams(collective_id=1, has_side_effects=True, vmem_limit_bytes=WHOLE),
        name="move_and_gather",
    )(
        queries.reshape(GROUPS, BLOCK, 2 * HALF), keys.reshape(GROUPS, BLOCK, 2 * KEYS_HALF),
        values.reshape(GROUPS, BLOCK, 2 * KEYS_HALF), output_gradient, group_shift.T, block_order, doc_lengths,
    )

    attn_full, dq_full, attn_send, dq_send, dkv = pl.pallas_call(
        attend_kernel,
        out_shape=(
            jax.ShapeDtypeStruct((ROWS, 2 * HALF), low),
            jax.ShapeDtypeStruct((ROWS, 2 * HALF), low),
            jax.ShapeDtypeStruct((ROWS, HALF), low),
            jax.ShapeDtypeStruct((ROWS, HALF), low),
            jax.ShapeDtypeStruct((SLOTS, BLOCK, 2 * KEYS_HALF), low),
        ),
        in_specs=[SMEM, SMEM, SMEM, ANY, ANY, ANY],
        out_specs=(ANY,) * 5,
        scratch_shapes=[
            pltpu.VMEM((2 * ROWS, HALF), low), pltpu.VMEM((2 * ROWS, HALF), low),
            pltpu.VMEM((SLOTS, BLOCK, 2 * KEYS_HALF), low),
            pltpu.VMEM((2 * ROWS, HALF), low), pltpu.VMEM((2 * ROWS, HALF), low),
            pltpu.VMEM((SLOTS, BLOCK, 2 * KEYS_HALF), low),
            pltpu.VMEM((GROUP_ROWS, 2 * KEYS_HALF), low),
            pltpu.VMEM((2, 2, HEAD, GROUP_ROWS), jnp.float32),
            pltpu.VMEM((GROUP_ROWS, 2 * KEYS_HALF), low),
            dma((2 + PIECES,)), dma((4 + PIECES,)),
        ],
        compiler_params=pltpu.CompilerParams(vmem_limit_bytes=WHOLE),
        name="attend",
    )(
        table, doc_lengths, block_order,
        rq.reshape(2 * ROWS, HALF), do2.reshape(2 * ROWS, HALF),
        kv.reshape(SLOTS, BLOCK, 2 * KEYS_HALF),
    )

    region = (2, ROWS, 2 * KEYS_HALF)
    attn_in, dq_in, grads = pl.pallas_call(
        scatter_kernel,
        out_shape=(
            jax.ShapeDtypeStruct((ROWS, HALF), low),
            jax.ShapeDtypeStruct((ROWS, HALF), low),
            jax.ShapeDtypeStruct(region, low),
        ),
        in_specs=[ANY, ANY, ANY],
        out_specs=(ANY, ANY, ANY),
        scratch_shapes=[
            pltpu.VMEM((CHIPS,) + region, low),
            pltpu.VMEM(region, low),
            pltpu.VMEM(region, low), pltpu.VMEM(region, low),
            pltpu.VMEM((2,) + region, low),
            pltpu.VMEM(region, low), pltpu.VMEM((2,) + region, low),
            pltpu.VMEM(region, low), pltpu.VMEM(region, low),
            pltpu.VMEM(region, low),
            dma((3,)), dma((3,)),
            dma((5,)), dma((5,)),
            dma((2, 2)), dma((2, 2)),
            dma((2,)), dma((2,)),
            dma((2, 3)), dma((2, 3)),
            dma, dma,
        ],
        compiler_params=pltpu.CompilerParams(collective_id=2, has_side_effects=True, vmem_limit_bytes=WHOLE),
        name="reduce_and_share",
    )(attn_send, dq_send, dkv.reshape((CHIPS,) + region))

    return pl.pallas_call(
        finish_kernel,
        out_shape=(
            jax.ShapeDtypeStruct((ROWS, 2 * HALF), low),
            jax.ShapeDtypeStruct((ROWS, 2 * HALF), low),
            jax.ShapeDtypeStruct((ROWS, 2 * KEYS_HALF), low),
            jax.ShapeDtypeStruct((ROWS, 2 * KEYS_HALF), low),
        ),
        in_specs=[ANY] * 5,
        out_specs=(ANY,) * 4,
        scratch_shapes=[pltpu.VMEM((2, ROWS, HALF), low), pltpu.VMEM(region, low), dma((3,)), dma((6,))],
        input_output_aliases={0: 0, 1: 1},
        compiler_params=pltpu.CompilerParams(vmem_limit_bytes=WHOLE),
        name="finish",
    )(attn_full, dq_full, attn_in, dq_in, grads)


def solution(mesh):
    rows = P(("dp", "fsdp"), None)
    return jax.shard_map(
        on_device,
        mesh=mesh,
        in_specs=(rows, rows, rows, rows, P(), P(), P()),
        out_specs=(rows, rows, rows, rows),
        check_vma=False,
    )
```

```python
import functools
import math

import jax
import jax.numpy as jnp
from jax import lax
from jax.experimental import pallas as pl
from jax.experimental.pallas import tpu as pltpu
from jax.sharding import PartitionSpec as P

HEADS = 32
KEY_HEADS = 4
HEAD = 128
PER_KEY = 8
BLOCK = 16
ROWS = 128
GROUPS = 8
MEMBERS = 16
CHIPS = 8
GROUP_ROWS = 2048
HALF = HEADS * HEAD // 2
KEYS_HALF = KEY_HEADS * HEAD // 2
CHUNK = 128
MOST_CHUNKS = 9
DOCS = 8
TOGETHER = 2
SLOTS = GROUPS * MEMBERS
PIECES = 4
SCALE = 1.0 / math.sqrt(HEAD)
LOG2E = 1.4426950408889634
FILL = -1e30
MESH = pl.DeviceIdType.MESH
WHOLE = 56 << 20


def place():
    group = lax.axis_index("dp")
    member = lax.axis_index("fsdp")
    return group, member // 8, (member // 2) % 4, member % 2


def member_of(zh, x, core):
    return zh * 8 + x * 2 + core


def gather_kernel(
    q_ref, k_ref, v_ref, do_ref, shift_hbm, order_hbm, lengths_hbm,
    rq_ref, do2_ref, kv_ref, table_ref,
    shift_ref, order_ref, lengths_ref, counts, k_in, v_in, q_in, send_q, send_kv, own,
    in_sem, kv_ssem, kv_rsem, q_ssem, q_rsem, do_ssem, do_rsem, o_ssem, o_rsem, c_sem, z_ssem, z_rsem, f_ssem, f_rsem, local_sem,
):
    group, zh, x, core = place()
    member = member_of(zh, x, core)
    chip = zh * 4 + x
    chip_z = (1 - zh) * 4 + x
    right, left = (x + 1) % 4, (x + 3) % 4
    other = 1 - core

    def peer(plane, col, side):
        return (group, member_of(plane, col, side))

    def remote(src, dst, ssem, rsem, dev):
        return pltpu.make_async_remote_copy(
            src_ref=src, dst_ref=dst, send_sem=ssem, recv_sem=rsem, device_id=dev, device_id_type=MESH
        )

    loads = [
        pltpu.make_async_copy(src, dst, in_sem.at[i])
        for i, (src, dst) in enumerate((
            (shift_hbm, shift_ref), (k_ref, k_in), (v_ref, v_in), (q_ref, q_in),
            (order_hbm, order_ref), (lengths_hbm, lengths_ref),
        ))
    ]
    for copy in loads:
        copy.start()

    def target(slot):
        return ((group // 4 + slot // 4) % 2) * 4 + (group % 4 + slot % 4) % 4

    def origin(slot):
        return ((group // 4 + slot // 4) % 2) * 4 + (group % 4 + 4 - slot % 4) % 4

    barrier = pltpu.get_barrier_semaphore()
    greeted = 0
    for slot in range(1, GROUPS):
        for side in range(2):
            dev = (origin(slot), member_of(zh, x, side))
            pl.semaphore_signal(barrier, inc=1, device_id=dev, device_id_type=MESH)
            greeted += 1
    around = [(1 - zh, x, 0), (1 - zh, x, 1)]
    for side in range(2):
        around += [(zh, right, side), (zh, left, side)]
    for spot in around + [(zh, x, other)]:
        pl.semaphore_signal(barrier, inc=1, device_id=peer(*spot), device_id_type=MESH)
        greeted += 1

    def block_for(row, step):
        found = jnp.int32(0)
        for b in range(GROUPS):
            found = jnp.maximum(found, jnp.where(shift_ref[b, row] == step, b, 0))
        return found

    loads[0].wait()
    blocks = [block_for(member, (target(slot) + GROUPS - group) % GROUPS) for slot in range(GROUPS)]
    loads[1].wait()
    loads[2].wait()
    for step in range(GROUPS):
        for side in range(2):
            cols = slice(side * KEYS_HALF, (side + 1) * KEYS_HALF)
            send_kv[side, step, :, 0:KEYS_HALF] = k_in[blocks[step], :, cols]
            send_kv[side, step, :, KEYS_HALF:] = v_in[blocks[step], :, cols]

    pl.semaphore_wait(barrier, greeted)
    own_kv = pltpu.make_async_copy(send_kv.at[:, 0], own.at[:, 0], local_sem.at[0])
    own_kv.start()
    kv_copies = [
        remote(send_kv.at[:, s], own.at[:, s], kv_ssem.at[s], kv_rsem.at[s], (target(s), member))
        for s in range(1, GROUPS)
    ]
    for copy in kv_copies:
        copy.start()
    loads[3].wait()
    for step in range(GROUPS):
        send_q[step] = q_in[blocks[step]]

    def halves(ref, side):
        return ref.at[:, pl.ds(pl.multiple_of(side * HALF, HALF), HALF)]

    def half_cols(ref, side):
        return ref.at[:, pl.ds(pl.multiple_of(side * HALF, HALF), HALF)]

    sends = []

    def go(copy):
        copy.start()
        sends.append(copy)
        return copy

    def q_send(slot, flip):
        side = core if flip == 0 else other
        return go(remote(
            half_cols(send_q.at[slot], side), rq_ref.at[core, slot],
            q_ssem.at[slot, flip], q_rsem.at[slot, flip], (target(slot), member_of(zh, x, side)),
        ))

    def own_send(index, flip, part, spot):
        side = core if flip == 0 else other
        some = pl.ds(part * 4, 4)
        return go(remote(
            own.at[side, some], kv_ref.at[chip, core, some],
            o_ssem.at[index, flip, part], o_rsem.at[index, flip, part], peer(*spot, side),
        ))

    own_kv.wait()
    own_z, own_r, own_l = {}, {}, {}
    arrived = 0
    for part in range(2):
        while arrived < (3, 7)[part]:
            kv_copies[arrived].wait_recv()
            arrived += 1
        for f in range(2):
            own_z[f, part] = own_send(0, f, part, (1 - zh, x))
            own_r[f, part] = own_send(1, f, part, (zh, right))
            own_l[f, part] = own_send(2, f, part, (zh, left))
    q_copies = [q_send(slot, flip) for slot in range(1, 4) for flip in range(2)]
    own_c = go(remote(own.at[other], kv_ref.at[chip, core], c_sem.at[0], c_sem.at[1], peer(zh, x, other)))
    own_here = pltpu.make_async_copy(own.at[core], kv_ref.at[chip, core], local_sem.at[1])
    own_here.start()
    q_copies.append(q_send(0, 1))
    q_here = pltpu.make_async_copy(half_cols(send_q.at[0], core), rq_ref.at[core, 0], local_sem.at[3])
    q_here.start()
    do_copy = go(remote(halves(do_ref, other), do2_ref.at[core], do_ssem, do_rsem, peer(zh, x, other)))
    own_do = pltpu.make_async_copy(halves(do_ref, core), do2_ref.at[core], local_sem.at[2])
    own_do.start()

    def came(copies, f):
        for part in range(2):
            copies[f, part].wait_recv()

    def fill(row, carry):
        for slot in range(GROUPS):
            b = block_for(row, (group + GROUPS - origin(slot)) % GROUPS)
            table_ref[row * GROUPS + slot] = order_ref[group, row * GROUPS + b]
        return carry

    loads[4].wait()
    loads[5].wait()
    lax.fori_loop(0, MEMBERS, fill, 0)
    for side in range(2):
        row = member_of(zh, x, side)
        for slot in range(GROUPS):
            b = block_for(row, (group + GROUPS - origin(slot)) % GROUPS)
            table_ref[128 + side * GROUPS + slot] = order_ref[group, row * GROUPS + b]
            table_ref[144 + side * GROUPS + slot] = b

    def count_chunks(index, carry):
        p = table_ref[128 + index] * BLOCK
        first = jnp.int32(0)
        end = jnp.int32(0)
        for e in range(DOCS):
            length = lengths_ref[group, e]
            end = end + length
            first = first + jnp.where(end <= p, length, 0)
        counts[index] = (p + BLOCK - 1) // CHUNK - first // CHUNK + 1
        return carry

    lax.fori_loop(0, 2 * GROUPS, count_chunks, 0)

    def rank_of(index, carry):
        mine = counts[index] * 16 + index
        rank = jnp.int32(0)
        for i in range(2 * GROUPS):
            rank = rank + jnp.where(counts[i] * 16 + i < mine, 1, 0)
        counts[16 + index] = rank
        return carry

    lax.fori_loop(0, 2 * GROUPS, rank_of, 0)

    def place_rank(rank, carry):
        found = jnp.int32(0)
        for i in range(2 * GROUPS):
            found = jnp.maximum(found, jnp.where(counts[16 + i] == rank, i, 0))
        table_ref[160 + rank] = found
        return carry

    lax.fori_loop(0, 2 * GROUPS, place_rank, 0)

    z_r, z_l = [None, None], [None, None]
    for f in range(2):
        came(own_z, f)
        src = kv_ref.at[chip_z, core if f == 0 else other]
        z_r[f] = go(remote(src, src, z_ssem.at[0, f], z_rsem.at[0, f], peer(zh, right, core)))
        z_l[f] = go(remote(src, src, z_ssem.at[1, f], z_rsem.at[1, f], peer(zh, left, core)))

    q_copies += [q_send(slot, flip) for slot in range(4, GROUPS) for flip in range(2)]
    came(own_r, 0)
    src = kv_ref.at[zh * 4 + left, core]
    far_r = go(remote(src, src, f_ssem.at[0, 0], f_rsem.at[0, 0], peer(zh, right, core)))
    came(own_l, 1)
    src = kv_ref.at[zh * 4 + right, other]
    far_l = go(remote(src, src, f_ssem.at[0, 1], f_rsem.at[0, 1], peer(zh, left, core)))
    came(own_r, 1)
    came(own_l, 0)
    z_r[0].wait_recv()
    src = kv_ref.at[(1 - zh) * 4 + left, core]
    zfar_r = go(remote(src, src, f_ssem.at[1, 0], f_rsem.at[1, 0], peer(zh, right, core)))
    z_l[1].wait_recv()
    src = kv_ref.at[(1 - zh) * 4 + right, other]
    zfar_l = go(remote(src, src, f_ssem.at[1, 1], f_rsem.at[1, 1], peer(zh, left, core)))

    z_r[1].wait_recv()
    z_l[0].wait_recv()
    own_c.wait_recv()
    do_copy.wait_recv()
    for copy in (far_r, far_l, zfar_r, zfar_l):
        copy.wait_recv()
    for copy in q_copies:
        copy.wait_recv()
    q_here.wait()
    own_do.wait()
    own_here.wait()
    for copy in kv_copies + sends:
        copy.wait_send()


def attend_kernel(
    table_ref, lengths_ref, order_ref, rq_hbm, do_hbm, kv_hbm,
    attn_full, dq_full, attn_send, dq_send, dkv_hbm,
    rq_ref, do_ref, kv_ref, attn_ref, dq_ref, dkv_ref, ks, acc, turned, in_sem, out_sem,
):
    group = lax.axis_index("dp")
    pieces = [pl.ds(i * SLOTS // PIECES, SLOTS // PIECES) for i in range(PIECES)]
    kv_loads = [
        pltpu.make_async_copy(kv_hbm.at[piece], kv_ref.at[piece], in_sem.at[2 + i]) for i, piece in enumerate(pieces)
    ]
    loads = [pltpu.make_async_copy(rq_hbm, rq_ref, in_sem.at[0]), pltpu.make_async_copy(do_hbm, do_ref, in_sem.at[1])]
    for copy in kv_loads + loads:
        copy.start()

    def arrange(slot, carry):
        dst = pl.multiple_of(table_ref[slot] * BLOCK, BLOCK)
        ks[pl.ds(dst, BLOCK), :] = kv_ref[slot]
        return carry

    acc[...] = jnp.zeros_like(acc)
    for i, copy in enumerate(kv_loads):
        copy.wait()
        lax.fori_loop(i * SLOTS // PIECES, (i + 1) * SLOTS // PIECES, arrange, 0, unroll=8)
    for copy in loads:
        copy.wait()

    def describe(index):
        p = table_ref[128 + index]
        out_row = pl.multiple_of((index // GROUPS) * ROWS + table_ref[144 + index] * BLOCK, BLOCK)
        in_row = pl.multiple_of(index * BLOCK, BLOCK)
        first = jnp.int32(0)
        end = jnp.int32(0)
        for e in range(DOCS):
            length = lengths_ref[group, e]
            end = end + length
            first = first + jnp.where(end <= p * BLOCK, length, 0)
        low = first // CHUNK
        count = (p * BLOCK + BLOCK - 1) // CHUNK - low + 1
        return p, in_row, out_row, low, count

    def tile(x, width):
        return (x.reshape(PER_KEY, BLOCK, width))

    def run(n, items):
        width = n * CHUNK
        lanes = lax.broadcasted_iota(jnp.int32, (BLOCK, CHUNK), 1)
        chains = []
        for p, in_row, out_row, low, count in items:
            pos = p * BLOCK + lax.broadcasted_iota(jnp.int32, (BLOCK, CHUNK), 0)
            start = jnp.zeros((BLOCK, CHUNK), jnp.int32)
            end = jnp.int32(0)
            for e in range(DOCS):
                length = lengths_ref[group, e]
                end = end + length
                start = start + jnp.where(end <= pos, length, 0)
            base = pl.multiple_of(jnp.minimum(low, GROUP_ROWS // CHUNK - n) * CHUNK, CHUNK)
            keys = pl.ds(base, width)
            parts = []
            for c in range(n):
                key = base + c * CHUNK + lanes
                parts.append(jnp.where((key >= start) & (key <= pos), 0.0, FILL).astype(jnp.float32))
            bias = jnp.concatenate(parts, axis=1) if n > 1 else parts[0]
            for h in range(2):
                def heads(ref, row):
                    return jnp.concatenate(
                        [ref[pl.ds(row, BLOCK), pl.ds((h * PER_KEY + g) * HEAD, HEAD)] for g in range(PER_KEY)], axis=0
                    )
                d = dict(h=h, keys=keys, bias=bias, out_row=out_row)
                d['q'] = heads(rq_ref, in_row)
                d['do'] = heads(do_ref, out_row)
                d['k'] = lambda d=d: ks[d['keys'], pl.ds(d['h'] * HEAD, HEAD)]
                d['v'] = lambda d=d: ks[d['keys'], pl.ds(KEYS_HALF + d['h'] * HEAD, HEAD)]
                chains.append(d)
        for d in chains:
            s = lax.dot_general(d['q'], d['k'](), (((1,), (1,)), ((), ())), preferred_element_type=jnp.float32)
            d['s'] = (tile(s, width) + d['bias'][None]).reshape(PER_KEY * BLOCK, width)
        for d in chains:
            d['top'] = jnp.max(d['s'], axis=1, keepdims=True)
        for d in chains:
            d['dp'] = lax.dot_general(d['do'], d['v'](), (((1,), (1,)), ((), ())), preferred_element_type=jnp.float32)
        for d in chains:
            w = jnp.exp2((d['s'] - d['top']) * (SCALE * LOG2E))
            d['w'] = w
            d['inv'] = 1.0 / jnp.sum(w, axis=1, keepdims=True)
            d['wl'] = w.astype(jnp.bfloat16)
        for d in chains:
            out = lax.dot_general(d['wl'], d['v'](), (((1,), (0,)), ((), ())), preferred_element_type=jnp.float32)
            d['out'] = (out * d['inv']).astype(jnp.bfloat16)
            dw = d['do'].astype(jnp.float32)
            d['delta'] = jnp.sum(dw * d['out'].astype(jnp.float32), axis=1, keepdims=True)
            d['qs'] = (d['q'].astype(jnp.float32) * (d['inv'] * SCALE)).astype(jnp.bfloat16)
            d['dos'] = (dw * d['inv']).astype(jnp.bfloat16)
        for d in chains:
            acc[d['h'], 1, :, d['keys']] += lax.dot_general(
                d['dos'], d['wl'], (((0,), (0,)), ((), ())), preferred_element_type=jnp.float32
            )
        for d in chains:
            d['ds'] = (d['w'] * (d['dp'] - d['delta'])).astype(jnp.bfloat16)
        for d in chains:
            gq = lax.dot_general(d['ds'], d['k'](), (((1,), (0,)), ((), ())), preferred_element_type=jnp.float32)
            d['gq'] = (gq * (d['inv'] * SCALE)).astype(jnp.bfloat16)
        for d in chains:
            acc[d['h'], 0, :, d['keys']] += lax.dot_general(
                d['qs'], d['ds'], (((0,), (0,)), ((), ())), preferred_element_type=jnp.float32
            )
        for d in chains:
            for g in range(PER_KEY):
                cols = pl.ds((d['h'] * PER_KEY + g) * HEAD, HEAD)
                attn_ref[pl.ds(d['out_row'], BLOCK), cols] = d['out'][g * BLOCK:(g + 1) * BLOCK]
                dq_ref[pl.ds(d['out_row'], BLOCK), cols] = d['gq'][g * BLOCK:(g + 1) * BLOCK]

    def item(step, carry):
        items = [describe(table_ref[160 + step * TOGETHER + i]) for i in range(TOGETHER)]
        count = items[0][4]
        for it in items[1:]:
            count = jnp.maximum(count, it[4])
        for n in range(1, MOST_CHUNKS + 1):
            pl.when(count == n)(functools.partial(run, n, items))
        return carry

    lax.fori_loop(0, 2 * GROUPS // TOGETHER, item, 0)
    core = lax.axis_index("fsdp") % 2
    cols = pl.ds(pl.multiple_of(core * HALF, HALF), HALF)
    kept = pl.ds(pl.multiple_of(core * ROWS, ROWS), ROWS)
    sent = pl.ds(pl.multiple_of((1 - core) * ROWS, ROWS), ROWS)
    stores = [
        pltpu.make_async_copy(attn_ref.at[sent], attn_send, out_sem.at[0]),
        pltpu.make_async_copy(dq_ref.at[sent], dq_send, out_sem.at[1]),
        pltpu.make_async_copy(attn_ref.at[kept], attn_full.at[:, cols], out_sem.at[2]),
        pltpu.make_async_copy(dq_ref.at[kept], dq_full.at[:, cols], out_sem.at[3]),
    ]
    for copy in stores:
        copy.start()

    def turn(c, carry):
        keys = pl.ds(pl.multiple_of(c * CHUNK, CHUNK), CHUNK)
        for h in range(2):
            for which in range(2):
                turned[keys, pl.ds(which * KEYS_HALF + h * HEAD, HEAD)] = acc[h, which, :, keys].T.astype(jnp.bfloat16)
        return carry

    lax.fori_loop(0, GROUP_ROWS // CHUNK, turn, 0, unroll=4)

    def restore(slot, carry):
        src = pl.multiple_of(order_ref[group, slot] * BLOCK, BLOCK)
        dkv_ref[slot] = turned[pl.ds(src, BLOCK), :]
        return carry

    for i, piece in enumerate(pieces):
        lax.fori_loop(i * SLOTS // PIECES, (i + 1) * SLOTS // PIECES, restore, 0, unroll=8)
        copy = pltpu.make_async_copy(dkv_ref.at[piece], dkv_hbm.at[piece], out_sem.at[4 + i])
        copy.start()
        stores.append(copy)
    for copy in stores:
        copy.wait()


def scatter_kernel(
    attn_send, dq_send, u_hbm,
    attn_ref, dq_ref, grads_ref,
    u_ref, z0_in, far_out, far_in, cross_in, near_out, near_in, z1_out, z1_in, total,
    o_ssem, o_rsem, z_ssem, z_rsem, f_ssem, f_rsem, c_ssem, c_rsem, n_ssem, n_rsem, local_sem, u_sem,
):
    u_load = pltpu.make_async_copy(u_hbm, u_ref, u_sem)
    u_load.start()
    group, zh, x, core = place()
    right, left, across = (x + 1) % 4, (x + 3) % 4, (x + 2) % 4
    other = 1 - core
    z_peer = (group, member_of(1 - zh, x, core))
    r_peer = (group, member_of(zh, right, core))
    l_peer = (group, member_of(zh, left, core))
    core_peer = (group, member_of(zh, x, other))
    barrier = pltpu.get_barrier_semaphore()
    for dev in (z_peer, r_peer, l_peer, core_peer):
        pl.semaphore_signal(barrier, inc=1, device_id=dev, device_id_type=MESH)
    pl.semaphore_wait(barrier, 4)
    sends = []

    def go(src, dst, ssem, rsem, dev):
        copy = pltpu.make_async_remote_copy(
            src_ref=src, dst_ref=dst, send_sem=ssem, recv_sem=rsem, device_id=dev, device_id_type=MESH
        )
        copy.start()
        sends.append(copy)
        return copy

    def wide(value):
        return value.astype(jnp.float32)

    here, there = zh * 4, (1 - zh) * 4
    sides = ((0, r_peer, right), (1, l_peer, left))
    parts = [pl.ds(i * ROWS // 2, ROWS // 2) for i in range(2)]
    z0 = {
        (q, d): go(
            u_hbm.at[there + across, d, parts[q]], z0_in.at[d, parts[q]], z_ssem.at[2 * q + d], z_rsem.at[2 * q + d], z_peer
        )
        for q in range(2) for d in range(2)
    }
    cross = [go(u_hbm.at[there + to], cross_in.at[d], c_ssem.at[d], c_rsem.at[d], dev) for d, dev, to in sides]
    outs = [
        go(src, dst, o_ssem.at[i], o_rsem.at[i], core_peer)
        for i, (src, dst) in enumerate(((attn_send, attn_ref), (dq_send, dq_ref)))
    ]
    u_load.wait()
    far, near = {}, []

    def send_far(q):
        for d, dev, to in sides:
            z0[q, d].wait_recv()
            far_out[d, parts[q]] = (wide(u_ref[here + across, d, parts[q]]) + wide(z0_in[d, parts[q]])).astype(jnp.bfloat16)
            far[q, d] = go(far_out.at[d, parts[q]], far_in.at[d, parts[q]], f_ssem.at[d, q], f_rsem.at[d, q], dev)

    send_far(0)
    for d, dev, to in sides:
        near.append(go(u_ref.at[here + to, 1 - d], near_in.at[d, 1 - d], n_ssem.at[d, 0], n_rsem.at[d, 0], dev))
    for copy in cross:
        copy.wait_recv()
    z1_out[...] = (wide(u_ref[there + x]) + wide(cross_in[0]) + wide(cross_in[1])).astype(jnp.bfloat16)
    z1 = go(z1_out, z1_in, z_ssem.at[4], z_rsem.at[4], z_peer)
    send_far(1)
    for q in range(2):
        for d, dev, to in sides:
            far[q, d].wait_recv()
            near_out[d, parts[q]] = (wide(u_ref[here + to, d, parts[q]]) + wide(far_in[d, parts[q]])).astype(jnp.bfloat16)
            near.append(go(
                near_out.at[d, parts[q]], near_in.at[d, d, parts[q]], n_ssem.at[d, 1 + q], n_rsem.at[d, 1 + q], dev
            ))
    z1.wait_recv()
    for copy in near:
        copy.wait_recv()

    def add_up(side):
        total[side] = (
            wide(u_ref[here + x, side]) + wide(z1_in[side]) + wide(near_in[0, side]) + wide(near_in[1, side])
        ).astype(jnp.bfloat16)

    add_up(other)
    last = go(total.at[other], grads_ref.at[core], o_ssem.at[2], o_rsem.at[2], core_peer)
    add_up(core)
    kept = pltpu.make_async_copy(total.at[core], grads_ref.at[core], local_sem)
    kept.start()
    for copy in outs:
        copy.wait_recv()
    last.wait_recv()
    kept.wait()
    for copy in sends:
        copy.wait_send()


def finish_kernel(
    attn_full, dq_full, attn_in, dq_in, grads_in, attn_ref, dq_ref, gk_ref, gv_ref, wide, narrow, in_sem, out_sem,
):
    core = lax.axis_index("fsdp") % 2

    def cols(ref, side, width):
        return ref.at[:, pl.ds(pl.multiple_of(side * width, width), width)]

    groups = [
        (grads_in, narrow, [
            (narrow.at[side, :, pl.ds(which * KEYS_HALF, KEYS_HALF)], cols(dst, side, KEYS_HALF))
            for side in range(2) for which, dst in enumerate((gk_ref, gv_ref))
        ]),
        (attn_in, wide.at[0], [(wide.at[0], cols(attn_ref, 1 - core, HALF))]),
        (dq_in, wide.at[1], [(wide.at[1], cols(dq_ref, 1 - core, HALF))]),
    ]
    loads = [pltpu.make_async_copy(src, here, in_sem.at[i]) for i, (src, here, _) in enumerate(groups)]
    for copy in loads:
        copy.start()
    stores = []
    for copy, (_, _, pairs) in zip(loads, groups):
        copy.wait()
        for src, dst in pairs:
            out = pltpu.make_async_copy(src, dst, out_sem.at[len(stores)])
            out.start()
            stores.append(out)
    for copy in stores:
        copy.wait()


VMEM = pl.BlockSpec(memory_space=pltpu.VMEM)
SMEM = pl.BlockSpec(memory_space=pltpu.SMEM)
ANY = pl.BlockSpec(memory_space=pl.ANY)
HBM = pl.BlockSpec(memory_space=pltpu.HBM)


def on_device(queries, keys, values, output_gradient, doc_lengths, block_order, group_shift):
    low = jnp.bfloat16
    dma = pltpu.SemaphoreType.DMA
    rq, do2, kv, table = pl.pallas_call(
        gather_kernel,
        out_shape=(
            jax.ShapeDtypeStruct((2, GROUPS, BLOCK, HALF), low),
            jax.ShapeDtypeStruct((2, ROWS, HALF), low),
            jax.ShapeDtypeStruct((CHIPS, 2, GROUPS, BLOCK, 2 * KEYS_HALF), low),
            jax.ShapeDtypeStruct((256,), jnp.int32),
        ),
        in_specs=[HBM] * 7,
        out_specs=(ANY, ANY, ANY, SMEM),
        scratch_shapes=[
            pltpu.SMEM((GROUPS, MEMBERS), jnp.int32),
            pltpu.SMEM((GROUPS, MEMBERS * GROUPS), jnp.int32),
            pltpu.SMEM((GROUPS, DOCS), jnp.int32),
            pltpu.SMEM((32,), jnp.int32),
            pltpu.VMEM((GROUPS, BLOCK, 2 * KEYS_HALF), low),
            pltpu.VMEM((GROUPS, BLOCK, 2 * KEYS_HALF), low),
            pltpu.VMEM((GROUPS, BLOCK, 2 * HALF), low),
            pltpu.VMEM((GROUPS, BLOCK, 2 * HALF), low),
            pltpu.VMEM((2, GROUPS, BLOCK, 2 * KEYS_HALF), low),
            pltpu.VMEM((2, GROUPS, BLOCK, 2 * KEYS_HALF), low),
            dma((6,)),
            dma((GROUPS,)), dma((GROUPS,)),
            dma((GROUPS, 2)), dma((GROUPS, 2)),
            dma, dma,
            dma((3, 2, 2)), dma((3, 2, 2)), dma((2,)),
            dma((2, 2)), dma((2, 2)),
            dma((2, 2)), dma((2, 2)),
            dma((5,)),
        ],
        compiler_params=pltpu.CompilerParams(collective_id=1, has_side_effects=True, vmem_limit_bytes=WHOLE),
        name="move_and_gather",
    )(
        queries.reshape(GROUPS, BLOCK, 2 * HALF), keys.reshape(GROUPS, BLOCK, 2 * KEYS_HALF),
        values.reshape(GROUPS, BLOCK, 2 * KEYS_HALF), output_gradient, group_shift.T, block_order, doc_lengths,
    )

    attn_full, dq_full, attn_send, dq_send, dkv = pl.pallas_call(
        attend_kernel,
        out_shape=(
            jax.ShapeDtypeStruct((ROWS, 2 * HALF), low),
            jax.ShapeDtypeStruct((ROWS, 2 * HALF), low),
            jax.ShapeDtypeStruct((ROWS, HALF), low),
            jax.ShapeDtypeStruct((ROWS, HALF), low),
            jax.ShapeDtypeStruct((SLOTS, BLOCK, 2 * KEYS_HALF), low),
        ),
        in_specs=[SMEM, SMEM, SMEM, ANY, ANY, ANY],
        out_specs=(ANY,) * 5,
        scratch_shapes=[
            pltpu.VMEM((2 * ROWS, HALF), low), pltpu.VMEM((2 * ROWS, HALF), low),
            pltpu.VMEM((SLOTS, BLOCK, 2 * KEYS_HALF), low),
            pltpu.VMEM((2 * ROWS, HALF), low), pltpu.VMEM((2 * ROWS, HALF), low),
            pltpu.VMEM((SLOTS, BLOCK, 2 * KEYS_HALF), low),
            pltpu.VMEM((GROUP_ROWS, 2 * KEYS_HALF), low),
            pltpu.VMEM((2, 2, HEAD, GROUP_ROWS), jnp.float32),
            pltpu.VMEM((GROUP_ROWS, 2 * KEYS_HALF), low),
            dma((2 + PIECES,)), dma((4 + PIECES,)),
        ],
        compiler_params=pltpu.CompilerParams(vmem_limit_bytes=WHOLE),
        name="attend",
    )(
        table, doc_lengths, block_order,
        rq.reshape(2 * ROWS, HALF), do2.reshape(2 * ROWS, HALF),
        kv.reshape(SLOTS, BLOCK, 2 * KEYS_HALF),
    )

    region = (2, ROWS, 2 * KEYS_HALF)
    attn_in, dq_in, grads = pl.pallas_call(
        scatter_kernel,
        out_shape=(
            jax.ShapeDtypeStruct((ROWS, HALF), low),
            jax.ShapeDtypeStruct((ROWS, HALF), low),
            jax.ShapeDtypeStruct(region, low),
        ),
        in_specs=[ANY, ANY, ANY],
        out_specs=(ANY, ANY, ANY),
        scratch_shapes=[
            pltpu.VMEM((CHIPS,) + region, low),
            pltpu.VMEM(region, low),
            pltpu.VMEM(region, low), pltpu.VMEM(region, low),
            pltpu.VMEM((2,) + region, low),
            pltpu.VMEM(region, low), pltpu.VMEM((2,) + region, low),
            pltpu.VMEM(region, low), pltpu.VMEM(region, low),
            pltpu.VMEM(region, low),
            dma((3,)), dma((3,)),
            dma((5,)), dma((5,)),
            dma((2, 2)), dma((2, 2)),
            dma((2,)), dma((2,)),
            dma((2, 3)), dma((2, 3)),
            dma, dma,
        ],
        compiler_params=pltpu.CompilerParams(collective_id=2, has_side_effects=True, vmem_limit_bytes=WHOLE),
        name="reduce_and_share",
    )(attn_send, dq_send, dkv.reshape((CHIPS,) + region))

    return pl.pallas_call(
        finish_kernel,
        out_shape=(
            jax.ShapeDtypeStruct((ROWS, 2 * HALF), low),
            jax.ShapeDtypeStruct((ROWS, 2 * HALF), low),
            jax.ShapeDtypeStruct((ROWS, 2 * KEYS_HALF), low),
            jax.ShapeDtypeStruct((ROWS, 2 * KEYS_HALF), low),
        ),
        in_specs=[ANY] * 5,
        out_specs=(ANY,) * 4,
        scratch_shapes=[pltpu.VMEM((2, ROWS, HALF), low), pltpu.VMEM(region, low), dma((3,)), dma((6,))],
        input_output_aliases={0: 0, 1: 1},
        compiler_params=pltpu.CompilerParams(vmem_limit_bytes=WHOLE),
        name="finish",
    )(attn_full, dq_full, attn_in, dq_in, grads)


def solution(mesh):
    rows = P(("dp", "fsdp"), None)
    return jax.shard_map(
        on_device,
        mesh=mesh,
        in_specs=(rows, rows, rows, rows, P(), P(), P()),
        out_specs=(rows, rows, rows, rows),
        check_vma=False,
    )
```

```python
import functools
import math

import jax
import jax.numpy as jnp
from jax import lax
from jax.experimental import pallas as pl
from jax.experimental.pallas import tpu as pltpu
from jax.sharding import PartitionSpec as P

HEADS = 32
KEY_HEADS = 4
HEAD = 128
PER_KEY = 8
BLOCK = 16
ROWS = 128
GROUPS = 8
MEMBERS = 16
CHIPS = 8
GROUP_ROWS = 2048
HALF = HEADS * HEAD // 2
KEYS_HALF = KEY_HEADS * HEAD // 2
CHUNK = 128
MOST_CHUNKS = 9
DOCS = 8
TOGETHER = 2
SLOTS = GROUPS * MEMBERS
PIECES = 4
SCALE = 1.0 / math.sqrt(HEAD)
LOG2E = 1.4426950408889634
FILL = -1e30
MESH = pl.DeviceIdType.MESH
WHOLE = 56 << 20


def place():
    group = lax.axis_index("dp")
    member = lax.axis_index("fsdp")
    return group, member // 8, (member // 2) % 4, member % 2


def member_of(zh, x, core):
    return zh * 8 + x * 2 + core


def gather_kernel(
    q_ref, k_ref, v_ref, do_ref, shift_hbm, order_hbm, lengths_hbm,
    rq_ref, do2_ref, kv_ref, table_ref,
    shift_ref, order_ref, lengths_ref, counts, k_in, v_in, q_in, send_q, send_kv, own,
    in_sem, kv_ssem, kv_rsem, q_ssem, q_rsem, do_ssem, do_rsem, o_ssem, o_rsem, c_sem, z_ssem, z_rsem, f_ssem, f_rsem, local_sem,
):
    group, zh, x, core = place()
    member = member_of(zh, x, core)
    chip = zh * 4 + x
    chip_z = (1 - zh) * 4 + x
    right, left = (x + 1) % 4, (x + 3) % 4
    other = 1 - core

    def peer(plane, col, side):
        return (group, member_of(plane, col, side))

    def remote(src, dst, ssem, rsem, dev):
        return pltpu.make_async_remote_copy(
            src_ref=src, dst_ref=dst, send_sem=ssem, recv_sem=rsem, device_id=dev, device_id_type=MESH
        )

    loads = [
        pltpu.make_async_copy(src, dst, in_sem.at[i])
        for i, (src, dst) in enumerate((
            (shift_hbm, shift_ref), (k_ref, k_in), (v_ref, v_in), (q_ref, q_in),
            (order_hbm, order_ref), (lengths_hbm, lengths_ref),
        ))
    ]
    for copy in loads:
        copy.start()

    def target(slot):
        return ((group // 4 + slot // 4) % 2) * 4 + (group % 4 + slot % 4) % 4

    def origin(slot):
        return ((group // 4 + slot // 4) % 2) * 4 + (group % 4 + 4 - slot % 4) % 4

    barrier = pltpu.get_barrier_semaphore()
    greeted = 0
    for slot in range(1, GROUPS):
        for side in range(2):
            dev = (origin(slot), member_of(zh, x, side))
            pl.semaphore_signal(barrier, inc=1, device_id=dev, device_id_type=MESH)
            greeted += 1
    around = [(1 - zh, x, 0), (1 - zh, x, 1)]
    for side in range(2):
        around += [(zh, right, side), (zh, left, side)]
    for spot in around + [(zh, x, other)]:
        pl.semaphore_signal(barrier, inc=1, device_id=peer(*spot), device_id_type=MESH)
        greeted += 1

    def block_for(row, step):
        found = jnp.int32(0)
        for b in range(GROUPS):
            found = jnp.maximum(found, jnp.where(shift_ref[b, row] == step, b, 0))
        return found

    loads[0].wait()
    blocks = [block_for(member, (target(slot) + GROUPS - group) % GROUPS) for slot in range(GROUPS)]
    loads[1].wait()
    loads[2].wait()
    for step in range(GROUPS):
        for side in range(2):
            cols = slice(side * KEYS_HALF, (side + 1) * KEYS_HALF)
            send_kv[side, step, :, 0:KEYS_HALF] = k_in[blocks[step], :, cols]
            send_kv[side, step, :, KEYS_HALF:] = v_in[blocks[step], :, cols]

    pl.semaphore_wait(barrier, greeted)
    own_kv = pltpu.make_async_copy(send_kv.at[:, 0], own.at[:, 0], local_sem.at[0])
    own_kv.start()
    kv_copies = [
        remote(send_kv.at[:, s], own.at[:, s], kv_ssem.at[s], kv_rsem.at[s], (target(s), member))
        for s in range(1, GROUPS)
    ]
    for copy in kv_copies:
        copy.start()
    loads[3].wait()
    for step in range(GROUPS):
        send_q[step] = q_in[blocks[step]]

    def halves(ref, side):
        return ref.at[:, pl.ds(pl.multiple_of(side * HALF, HALF), HALF)]

    def half_cols(ref, side):
        return ref.at[:, pl.ds(pl.multiple_of(side * HALF, HALF), HALF)]

    sends = []

    def go(copy):
        copy.start()
        sends.append(copy)
        return copy

    def q_send(slot, flip):
        side = core if flip == 0 else other
        return go(remote(
            half_cols(send_q.at[slot], side), rq_ref.at[core, slot],
            q_ssem.at[slot, flip], q_rsem.at[slot, flip], (target(slot), member_of(zh, x, side)),
        ))

    def own_send(index, flip, part, spot):
        side = core if flip == 0 else other
        some = pl.ds(part * 4, 4)
        return go(remote(
            own.at[side, some], kv_ref.at[chip, core, some],
            o_ssem.at[index, flip, part], o_rsem.at[index, flip, part], peer(*spot, side),
        ))

    own_kv.wait()
    own_z, own_r, own_l = {}, {}, {}
    arrived = 0
    for part in range(2):
        while arrived < (3, 7)[part]:
            kv_copies[arrived].wait_recv()
            arrived += 1
        for f in range(2):
            own_r[f, part] = own_send(1, f, part, (zh, right))
            own_l[f, part] = own_send(2, f, part, (zh, left))
            own_z[f, part] = own_send(0, f, part, (1 - zh, x))
    q_copies = [q_send(slot, flip) for slot in range(1, 4) for flip in range(2)]
    own_c = go(remote(own.at[other], kv_ref.at[chip, core], c_sem.at[0], c_sem.at[1], peer(zh, x, other)))
    own_here = pltpu.make_async_copy(own.at[core], kv_ref.at[chip, core], local_sem.at[1])
    own_here.start()
    q_copies.append(q_send(0, 1))
    q_here = pltpu.make_async_copy(half_cols(send_q.at[0], core), rq_ref.at[core, 0], local_sem.at[3])
    q_here.start()
    do_copy = go(remote(halves(do_ref, other), do2_ref.at[core], do_ssem, do_rsem, peer(zh, x, other)))
    own_do = pltpu.make_async_copy(halves(do_ref, core), do2_ref.at[core], local_sem.at[2])
    own_do.start()

    def came(copies, f):
        for part in range(2):
            copies[f, part].wait_recv()

    def fill(row, carry):
        for slot in range(GROUPS):
            b = block_for(row, (group + GROUPS - origin(slot)) % GROUPS)
            table_ref[row * GROUPS + slot] = order_ref[group, row * GROUPS + b]
        return carry

    loads[4].wait()
    loads[5].wait()
    lax.fori_loop(0, MEMBERS, fill, 0)
    for side in range(2):
        row = member_of(zh, x, side)
        for slot in range(GROUPS):
            b = block_for(row, (group + GROUPS - origin(slot)) % GROUPS)
            table_ref[128 + side * GROUPS + slot] = order_ref[group, row * GROUPS + b]
            table_ref[144 + side * GROUPS + slot] = b

    def count_chunks(index, carry):
        p = table_ref[128 + index] * BLOCK
        first = jnp.int32(0)
        end = jnp.int32(0)
        for e in range(DOCS):
            length = lengths_ref[group, e]
            end = end + length
            first = first + jnp.where(end <= p, length, 0)
        counts[index] = (p + BLOCK - 1) // CHUNK - first // CHUNK + 1
        return carry

    lax.fori_loop(0, 2 * GROUPS, count_chunks, 0)

    def rank_of(index, carry):
        mine = counts[index] * 16 + index
        rank = jnp.int32(0)
        for i in range(2 * GROUPS):
            rank = rank + jnp.where(counts[i] * 16 + i < mine, 1, 0)
        counts[16 + index] = rank
        return carry

    lax.fori_loop(0, 2 * GROUPS, rank_of, 0)

    def place_rank(rank, carry):
        found = jnp.int32(0)
        for i in range(2 * GROUPS):
            found = jnp.maximum(found, jnp.where(counts[16 + i] == rank, i, 0))
        table_ref[160 + rank] = found
        return carry

    lax.fori_loop(0, 2 * GROUPS, place_rank, 0)

    z_r, z_l = [None, None], [None, None]
    for f in range(2):
        came(own_z, f)
        src = kv_ref.at[chip_z, core if f == 0 else other]
        z_r[f] = go(remote(src, src, z_ssem.at[0, f], z_rsem.at[0, f], peer(zh, right, core)))
        z_l[f] = go(remote(src, src, z_ssem.at[1, f], z_rsem.at[1, f], peer(zh, left, core)))

    q_copies += [q_send(slot, flip) for slot in range(4, GROUPS) for flip in range(2)]
    came(own_r, 0)
    src = kv_ref.at[zh * 4 + left, core]
    far_r = go(remote(src, src, f_ssem.at[0, 0], f_rsem.at[0, 0], peer(zh, right, core)))
    came(own_l, 1)
    src = kv_ref.at[zh * 4 + right, other]
    far_l = go(remote(src, src, f_ssem.at[0, 1], f_rsem.at[0, 1], peer(zh, left, core)))
    came(own_r, 1)
    came(own_l, 0)
    z_r[0].wait_recv()
    src = kv_ref.at[(1 - zh) * 4 + left, core]
    zfar_r = go(remote(src, src, f_ssem.at[1, 0], f_rsem.at[1, 0], peer(zh, right, core)))
    z_l[1].wait_recv()
    src = kv_ref.at[(1 - zh) * 4 + right, other]
    zfar_l = go(remote(src, src, f_ssem.at[1, 1], f_rsem.at[1, 1], peer(zh, left, core)))

    z_r[1].wait_recv()
    z_l[0].wait_recv()
    own_c.wait_recv()
    do_copy.wait_recv()
    for copy in (far_r, far_l, zfar_r, zfar_l):
        copy.wait_recv()
    for copy in q_copies:
        copy.wait_recv()
    q_here.wait()
    own_do.wait()
    own_here.wait()
    for copy in kv_copies + sends:
        copy.wait_send()


def attend_kernel(
    table_ref, lengths_ref, order_ref, rq_hbm, do_hbm, kv_hbm,
    attn_full, dq_full, attn_send, dq_send, dkv_hbm,
    rq_ref, do_ref, kv_ref, attn_ref, dq_ref, dkv_ref, ks, acc, turned, in_sem, out_sem,
):
    group = lax.axis_index("dp")
    pieces = [pl.ds(i * SLOTS // PIECES, SLOTS // PIECES) for i in range(PIECES)]
    kv_loads = [
        pltpu.make_async_copy(kv_hbm.at[piece], kv_ref.at[piece], in_sem.at[2 + i]) for i, piece in enumerate(pieces)
    ]
    loads = [pltpu.make_async_copy(rq_hbm, rq_ref, in_sem.at[0]), pltpu.make_async_copy(do_hbm, do_ref, in_sem.at[1])]
    for copy in kv_loads + loads:
        copy.start()

    def arrange(slot, carry):
        dst = pl.multiple_of(table_ref[slot] * BLOCK, BLOCK)
        ks[pl.ds(dst, BLOCK), :] = kv_ref[slot]
        return carry

    acc[...] = jnp.zeros_like(acc)
    for i, copy in enumerate(kv_loads):
        copy.wait()
        lax.fori_loop(i * SLOTS // PIECES, (i + 1) * SLOTS // PIECES, arrange, 0, unroll=8)
    for copy in loads:
        copy.wait()

    def describe(index):
        p = table_ref[128 + index]
        out_row = pl.multiple_of((index // GROUPS) * ROWS + table_ref[144 + index] * BLOCK, BLOCK)
        in_row = pl.multiple_of(index * BLOCK, BLOCK)
        first = jnp.int32(0)
        end = jnp.int32(0)
        for e in range(DOCS):
            length = lengths_ref[group, e]
            end = end + length
            first = first + jnp.where(end <= p * BLOCK, length, 0)
        low = first // CHUNK
        count = (p * BLOCK + BLOCK - 1) // CHUNK - low + 1
        return p, in_row, out_row, low, count

    def tile(x, width):
        return (x.reshape(PER_KEY, BLOCK, width))

    def run(n, items):
        width = n * CHUNK
        lanes = lax.broadcasted_iota(jnp.int32, (BLOCK, CHUNK), 1)
        chains = []
        for p, in_row, out_row, low, count in items:
            pos = p * BLOCK + lax.broadcasted_iota(jnp.int32, (BLOCK, CHUNK), 0)
            start = jnp.zeros((BLOCK, CHUNK), jnp.int32)
            end = jnp.int32(0)
            for e in range(DOCS):
                length = lengths_ref[group, e]
                end = end + length
                start = start + jnp.where(end <= pos, length, 0)
            base = pl.multiple_of(jnp.minimum(low, GROUP_ROWS // CHUNK - n) * CHUNK, CHUNK)
            keys = pl.ds(base, width)
            parts = []
            for c in range(n):
                key = base + c * CHUNK + lanes
                parts.append(jnp.where((key >= start) & (key <= pos), 0.0, FILL).astype(jnp.float32))
            bias = jnp.concatenate(parts, axis=1) if n > 1 else parts[0]
            for h in range(2):
                def heads(ref, row):
                    return jnp.concatenate(
                        [ref[pl.ds(row, BLOCK), pl.ds((h * PER_KEY + g) * HEAD, HEAD)] for g in range(PER_KEY)], axis=0
                    )
                d = dict(h=h, keys=keys, bias=bias, out_row=out_row)
                d['q'] = heads(rq_ref, in_row)
                d['do'] = heads(do_ref, out_row)
                d['k'] = lambda d=d: ks[d['keys'], pl.ds(d['h'] * HEAD, HEAD)]
                d['v'] = lambda d=d: ks[d['keys'], pl.ds(KEYS_HALF + d['h'] * HEAD, HEAD)]
                chains.append(d)
        for d in chains:
            s = lax.dot_general(d['q'], d['k'](), (((1,), (1,)), ((), ())), preferred_element_type=jnp.float32)
            d['s'] = (tile(s, width) + d['bias'][None]).reshape(PER_KEY * BLOCK, width)
        for d in chains:
            d['top'] = jnp.max(d['s'], axis=1, keepdims=True)
        for d in chains:
            d['dp'] = lax.dot_general(d['do'], d['v'](), (((1,), (1,)), ((), ())), preferred_element_type=jnp.float32)
        for d in chains:
            w = jnp.exp2((d['s'] - d['top']) * (SCALE * LOG2E))
            d['w'] = w
            d['inv'] = 1.0 / jnp.sum(w, axis=1, keepdims=True)
            d['wl'] = w.astype(jnp.bfloat16)
        for d in chains:
            out = lax.dot_general(d['wl'], d['v'](), (((1,), (0,)), ((), ())), preferred_element_type=jnp.float32)
            d['out'] = (out * d['inv']).astype(jnp.bfloat16)
            dw = d['do'].astype(jnp.float32)
            d['delta'] = jnp.sum(dw * d['out'].astype(jnp.float32), axis=1, keepdims=True)
            d['qs'] = (d['q'].astype(jnp.float32) * (d['inv'] * SCALE)).astype(jnp.bfloat16)
            d['dos'] = (dw * d['inv']).astype(jnp.bfloat16)
        for d in chains:
            acc[d['h'], 1, :, d['keys']] += lax.dot_general(
                d['dos'], d['wl'], (((0,), (0,)), ((), ())), preferred_element_type=jnp.float32
            )
        for d in chains:
            d['ds'] = d['wl'] * (d['dp'] - d['delta']).astype(jnp.bfloat16)
        for d in chains:
            gq = lax.dot_general(d['ds'], d['k'](), (((1,), (0,)), ((), ())), preferred_element_type=jnp.float32)
            d['gq'] = (gq * (d['inv'] * SCALE)).astype(jnp.bfloat16)
        for d in chains:
            acc[d['h'], 0, :, d['keys']] += lax.dot_general(
                d['qs'], d['ds'], (((0,), (0,)), ((), ())), preferred_element_type=jnp.float32
            )
        for d in chains:
            for g in range(PER_KEY):
                cols = pl.ds((d['h'] * PER_KEY + g) * HEAD, HEAD)
                attn_ref[pl.ds(d['out_row'], BLOCK), cols] = d['out'][g * BLOCK:(g + 1) * BLOCK]
                dq_ref[pl.ds(d['out_row'], BLOCK), cols] = d['gq'][g * BLOCK:(g + 1) * BLOCK]

    def item(step, carry):
        items = [describe(table_ref[160 + step * TOGETHER + i]) for i in range(TOGETHER)]
        count = items[0][4]
        for it in items[1:]:
            count = jnp.maximum(count, it[4])
        for n in range(1, MOST_CHUNKS + 1):
            pl.when(count == n)(functools.partial(run, n, items))
        return carry

    lax.fori_loop(0, 2 * GROUPS // TOGETHER, item, 0)
    core = lax.axis_index("fsdp") % 2
    cols = pl.ds(pl.multiple_of(core * HALF, HALF), HALF)
    kept = pl.ds(pl.multiple_of(core * ROWS, ROWS), ROWS)
    sent = pl.ds(pl.multiple_of((1 - core) * ROWS, ROWS), ROWS)
    stores = [
        pltpu.make_async_copy(attn_ref.at[sent], attn_send, out_sem.at[0]),
        pltpu.make_async_copy(dq_ref.at[sent], dq_send, out_sem.at[1]),
        pltpu.make_async_copy(attn_ref.at[kept], attn_full.at[:, cols], out_sem.at[2]),
        pltpu.make_async_copy(dq_ref.at[kept], dq_full.at[:, cols], out_sem.at[3]),
    ]
    for copy in stores:
        copy.start()

    def turn(c, carry):
        keys = pl.ds(pl.multiple_of(c * CHUNK, CHUNK), CHUNK)
        for h in range(2):
            for which in range(2):
                turned[keys, pl.ds(which * KEYS_HALF + h * HEAD, HEAD)] = acc[h, which, :, keys].T.astype(jnp.bfloat16)
        return carry

    lax.fori_loop(0, GROUP_ROWS // CHUNK, turn, 0, unroll=4)

    def restore(slot, carry):
        src = pl.multiple_of(order_ref[group, slot] * BLOCK, BLOCK)
        dkv_ref[slot] = turned[pl.ds(src, BLOCK), :]
        return carry

    for i, piece in enumerate(pieces):
        lax.fori_loop(i * SLOTS // PIECES, (i + 1) * SLOTS // PIECES, restore, 0, unroll=8)
        copy = pltpu.make_async_copy(dkv_ref.at[piece], dkv_hbm.at[piece], out_sem.at[4 + i])
        copy.start()
        stores.append(copy)
    for copy in stores:
        copy.wait()


def scatter_kernel(
    attn_send, dq_send, u_hbm,
    attn_ref, dq_ref, grads_ref,
    u_ref, z0_in, far_out, far_in, cross_in, near_out, near_in, z1_out, z1_in, total,
    o_ssem, o_rsem, z_ssem, z_rsem, f_ssem, f_rsem, c_ssem, c_rsem, n_ssem, n_rsem, local_sem, u_sem,
):
    u_load = pltpu.make_async_copy(u_hbm, u_ref, u_sem)
    u_load.start()
    group, zh, x, core = place()
    right, left, across = (x + 1) % 4, (x + 3) % 4, (x + 2) % 4
    other = 1 - core
    z_peer = (group, member_of(1 - zh, x, core))
    r_peer = (group, member_of(zh, right, core))
    l_peer = (group, member_of(zh, left, core))
    core_peer = (group, member_of(zh, x, other))
    barrier = pltpu.get_barrier_semaphore()
    for dev in (z_peer, r_peer, l_peer, core_peer):
        pl.semaphore_signal(barrier, inc=1, device_id=dev, device_id_type=MESH)
    pl.semaphore_wait(barrier, 4)
    sends = []

    def go(src, dst, ssem, rsem, dev):
        copy = pltpu.make_async_remote_copy(
            src_ref=src, dst_ref=dst, send_sem=ssem, recv_sem=rsem, device_id=dev, device_id_type=MESH
        )
        copy.start()
        sends.append(copy)
        return copy

    def wide(value):
        return value.astype(jnp.float32)

    here, there = zh * 4, (1 - zh) * 4
    sides = ((0, r_peer, right), (1, l_peer, left))
    parts = [pl.ds(i * ROWS // 2, ROWS // 2) for i in range(2)]
    z0 = {
        (q, d): go(
            u_hbm.at[there + across, d, parts[q]], z0_in.at[d, parts[q]], z_ssem.at[2 * q + d], z_rsem.at[2 * q + d], z_peer
        )
        for q in range(2) for d in range(2)
    }
    cross = [go(u_hbm.at[there + to], cross_in.at[d], c_ssem.at[d], c_rsem.at[d], dev) for d, dev, to in sides]
    outs = [
        go(src, dst, o_ssem.at[i], o_rsem.at[i], core_peer)
        for i, (src, dst) in enumerate(((attn_send, attn_ref), (dq_send, dq_ref)))
    ]
    u_load.wait()
    far, near = {}, []

    def send_far(q):
        for d, dev, to in sides:
            z0[q, d].wait_recv()
            far_out[d, parts[q]] = (wide(u_ref[here + across, d, parts[q]]) + wide(z0_in[d, parts[q]])).astype(jnp.bfloat16)
            far[q, d] = go(far_out.at[d, parts[q]], far_in.at[d, parts[q]], f_ssem.at[d, q], f_rsem.at[d, q], dev)

    send_far(0)
    for d, dev, to in sides:
        near.append(go(u_ref.at[here + to, 1 - d], near_in.at[d, 1 - d], n_ssem.at[d, 0], n_rsem.at[d, 0], dev))
    for copy in cross:
        copy.wait_recv()
    z1_out[...] = (wide(u_ref[there + x]) + wide(cross_in[0]) + wide(cross_in[1])).astype(jnp.bfloat16)
    z1 = go(z1_out, z1_in, z_ssem.at[4], z_rsem.at[4], z_peer)
    send_far(1)
    for q in range(2):
        for d, dev, to in sides:
            far[q, d].wait_recv()
            near_out[d, parts[q]] = (wide(u_ref[here + to, d, parts[q]]) + wide(far_in[d, parts[q]])).astype(jnp.bfloat16)
            near.append(go(
                near_out.at[d, parts[q]], near_in.at[d, d, parts[q]], n_ssem.at[d, 1 + q], n_rsem.at[d, 1 + q], dev
            ))
    z1.wait_recv()
    for copy in near:
        copy.wait_recv()

    def add_up(side):
        total[side] = (
            wide(u_ref[here + x, side]) + wide(z1_in[side]) + wide(near_in[0, side]) + wide(near_in[1, side])
        ).astype(jnp.bfloat16)

    add_up(other)
    last = go(total.at[other], grads_ref.at[core], o_ssem.at[2], o_rsem.at[2], core_peer)
    add_up(core)
    kept = pltpu.make_async_copy(total.at[core], grads_ref.at[core], local_sem)
    kept.start()
    for copy in outs:
        copy.wait_recv()
    last.wait_recv()
    kept.wait()
    for copy in sends:
        copy.wait_send()


def finish_kernel(
    attn_full, dq_full, attn_in, dq_in, grads_in, attn_ref, dq_ref, gk_ref, gv_ref, wide, narrow, in_sem, out_sem,
):
    core = lax.axis_index("fsdp") % 2

    def cols(ref, side, width):
        return ref.at[:, pl.ds(pl.multiple_of(side * width, width), width)]

    groups = [
        (grads_in, narrow, [
            (narrow.at[side, :, pl.ds(which * KEYS_HALF, KEYS_HALF)], cols(dst, side, KEYS_HALF))
            for side in range(2) for which, dst in enumerate((gk_ref, gv_ref))
        ]),
        (attn_in, wide.at[0], [(wide.at[0], cols(attn_ref, 1 - core, HALF))]),
        (dq_in, wide.at[1], [(wide.at[1], cols(dq_ref, 1 - core, HALF))]),
    ]
    loads = [pltpu.make_async_copy(src, here, in_sem.at[i]) for i, (src, here, _) in enumerate(groups)]
    for copy in loads:
        copy.start()
    stores = []
    for copy, (_, _, pairs) in zip(loads, groups):
        copy.wait()
        for src, dst in pairs:
            out = pltpu.make_async_copy(src, dst, out_sem.at[len(stores)])
            out.start()
            stores.append(out)
    for copy in stores:
        copy.wait()


VMEM = pl.BlockSpec(memory_space=pltpu.VMEM)
SMEM = pl.BlockSpec(memory_space=pltpu.SMEM)
ANY = pl.BlockSpec(memory_space=pl.ANY)
HBM = pl.BlockSpec(memory_space=pltpu.HBM)


def on_device(queries, keys, values, output_gradient, doc_lengths, block_order, group_shift):
    low = jnp.bfloat16
    dma = pltpu.SemaphoreType.DMA
    rq, do2, kv, table = pl.pallas_call(
        gather_kernel,
        out_shape=(
            jax.ShapeDtypeStruct((2, GROUPS, BLOCK, HALF), low),
            jax.ShapeDtypeStruct((2, ROWS, HALF), low),
            jax.ShapeDtypeStruct((CHIPS, 2, GROUPS, BLOCK, 2 * KEYS_HALF), low),
            jax.ShapeDtypeStruct((256,), jnp.int32),
        ),
        in_specs=[HBM] * 7,
        out_specs=(ANY, ANY, ANY, SMEM),
        scratch_shapes=[
            pltpu.SMEM((GROUPS, MEMBERS), jnp.int32),
            pltpu.SMEM((GROUPS, MEMBERS * GROUPS), jnp.int32),
            pltpu.SMEM((GROUPS, DOCS), jnp.int32),
            pltpu.SMEM((32,), jnp.int32),
            pltpu.VMEM((GROUPS, BLOCK, 2 * KEYS_HALF), low),
            pltpu.VMEM((GROUPS, BLOCK, 2 * KEYS_HALF), low),
            pltpu.VMEM((GROUPS, BLOCK, 2 * HALF), low),
            pltpu.VMEM((GROUPS, BLOCK, 2 * HALF), low),
            pltpu.VMEM((2, GROUPS, BLOCK, 2 * KEYS_HALF), low),
            pltpu.VMEM((2, GROUPS, BLOCK, 2 * KEYS_HALF), low),
            dma((6,)),
            dma((GROUPS,)), dma((GROUPS,)),
            dma((GROUPS, 2)), dma((GROUPS, 2)),
            dma, dma,
            dma((3, 2, 2)), dma((3, 2, 2)), dma((2,)),
            dma((2, 2)), dma((2, 2)),
            dma((2, 2)), dma((2, 2)),
            dma((5,)),
        ],
        compiler_params=pltpu.CompilerParams(collective_id=1, has_side_effects=True, vmem_limit_bytes=WHOLE),
        name="move_and_gather",
    )(
        queries.reshape(GROUPS, BLOCK, 2 * HALF), keys.reshape(GROUPS, BLOCK, 2 * KEYS_HALF),
        values.reshape(GROUPS, BLOCK, 2 * KEYS_HALF), output_gradient, group_shift.T, block_order, doc_lengths,
    )

    attn_full, dq_full, attn_send, dq_send, dkv = pl.pallas_call(
        attend_kernel,
        out_shape=(
            jax.ShapeDtypeStruct((ROWS, 2 * HALF), low),
            jax.ShapeDtypeStruct((ROWS, 2 * HALF), low),
            jax.ShapeDtypeStruct((ROWS, HALF), low),
            jax.ShapeDtypeStruct((ROWS, HALF), low),
            jax.ShapeDtypeStruct((SLOTS, BLOCK, 2 * KEYS_HALF), low),
        ),
        in_specs=[SMEM, SMEM, SMEM, ANY, ANY, ANY],
        out_specs=(ANY,) * 5,
        scratch_shapes=[
            pltpu.VMEM((2 * ROWS, HALF), low), pltpu.VMEM((2 * ROWS, HALF), low),
            pltpu.VMEM((SLOTS, BLOCK, 2 * KEYS_HALF), low),
            pltpu.VMEM((2 * ROWS, HALF), low), pltpu.VMEM((2 * ROWS, HALF), low),
            pltpu.VMEM((SLOTS, BLOCK, 2 * KEYS_HALF), low),
            pltpu.VMEM((GROUP_ROWS, 2 * KEYS_HALF), low),
            pltpu.VMEM((2, 2, HEAD, GROUP_ROWS), jnp.float32),
            pltpu.VMEM((GROUP_ROWS, 2 * KEYS_HALF), low),
            dma((2 + PIECES,)), dma((4 + PIECES,)),
        ],
        compiler_params=pltpu.CompilerParams(vmem_limit_bytes=WHOLE),
        name="attend",
    )(
        table, doc_lengths, block_order,
        rq.reshape(2 * ROWS, HALF), do2.reshape(2 * ROWS, HALF),
        kv.reshape(SLOTS, BLOCK, 2 * KEYS_HALF),
    )

    region = (2, ROWS, 2 * KEYS_HALF)
    attn_in, dq_in, grads = pl.pallas_call(
        scatter_kernel,
        out_shape=(
            jax.ShapeDtypeStruct((ROWS, HALF), low),
            jax.ShapeDtypeStruct((ROWS, HALF), low),
            jax.ShapeDtypeStruct(region, low),
        ),
        in_specs=[ANY, ANY, ANY],
        out_specs=(ANY, ANY, ANY),
        scratch_shapes=[
            pltpu.VMEM((CHIPS,) + region, low),
            pltpu.VMEM(region, low),
            pltpu.VMEM(region, low), pltpu.VMEM(region, low),
            pltpu.VMEM((2,) + region, low),
            pltpu.VMEM(region, low), pltpu.VMEM((2,) + region, low),
            pltpu.VMEM(region, low), pltpu.VMEM(region, low),
            pltpu.VMEM(region, low),
            dma((3,)), dma((3,)),
            dma((5,)), dma((5,)),
            dma((2, 2)), dma((2, 2)),
            dma((2,)), dma((2,)),
            dma((2, 3)), dma((2, 3)),
            dma, dma,
        ],
        compiler_params=pltpu.CompilerParams(collective_id=2, has_side_effects=True, vmem_limit_bytes=WHOLE),
        name="reduce_and_share",
    )(attn_send, dq_send, dkv.reshape((CHIPS,) + region))

    return pl.pallas_call(
        finish_kernel,
        out_shape=(
            jax.ShapeDtypeStruct((ROWS, 2 * HALF), low),
            jax.ShapeDtypeStruct((ROWS, 2 * HALF), low),
            jax.ShapeDtypeStruct((ROWS, 2 * KEYS_HALF), low),
            jax.ShapeDtypeStruct((ROWS, 2 * KEYS_HALF), low),
        ),
        in_specs=[ANY] * 5,
        out_specs=(ANY,) * 4,
        scratch_shapes=[pltpu.VMEM((2, ROWS, HALF), low), pltpu.VMEM(region, low), dma((3,)), dma((6,))],
        input_output_aliases={0: 0, 1: 1},
        compiler_params=pltpu.CompilerParams(vmem_limit_bytes=WHOLE),
        name="finish",
    )(attn_full, dq_full, attn_in, dq_in, grads)


def solution(mesh):
    rows = P(("dp", "fsdp"), None)
    return jax.shard_map(
        on_device,
        mesh=mesh,
        in_specs=(rows, rows, rows, rows, P(), P(), P()),
        out_specs=(rows, rows, rows, rows),
        check_vma=False,
    )
```
